32 devices in a mesh: row: 8 (over z, x), col: 4 (over y, core).
Axes of the slice: x: 2, y: 2, z: 4, core: 2. Of those that a mesh axis runs over, the one named last changes fastest.
Arguments:
- schur: float32 [2, 8192, 4096], P(None, 'row', 'col'), may hold values from -6 to 6
- lower: bfloat16 [2, 8192, 2048], P(None, 'row', 'col'), may hold values from -6 to 6
- upper: bfloat16 [2, 2048, 4096], P(None, 'row', 'col'), may hold values from -0.1875 to 0.1875
- tile_mask: int32 [2, 64, 16], P(None, 'row', 'col'), may hold values from 0 to 1, as said below
- row_map: int32 [2, 8192], P(None, 'row'), may hold values from 0 to 8191, as said below
- front: float32 [8192, 4096], P('row', 'col'), may hold values from -6 to 6
Outputs:
- front_out: float32 [8192, 4096], P('row', 'col')
The draws below stay inside these ranges and needn't reach their ends.
Inputs may be any that keep to these rules, and one draw needn't show every extreme that they name: `tile_mask`: in every row of tiles of each child, each aligned pair of tile columns (2 j, 2 j + 1) holds exactly one 1. `row_map`: for each child a permutation of the 8192 rows. Of the 1024 rows of any aligned block, at least 64 and at most 192 map into any one aligned block of 1024 parent rows; some pair of blocks reaches 192.
All inputs are finite; a program needn't handle non-finite values.
Results may differ from the reference program's by a relative error of at most 0.0003.
Values may be sent and summed in bfloat16 or wider, within the bound.
No kernel may reach another device: no remote copies, remote signals or barrier semaphores. Data moves between devices by JAX's collectives and lax.ppermute only.
A program may use at most 128 MiB of HBM per device.

```python
import jax
import jax.numpy as jnp

W = 4096
K = 2048
TILE = 128
CHILDREN = 2
ROWS_DEV = 1024
M = 8192


def draw_tile_mask(key, part):
    picks = jax.random.randint(key, (2, M // TILE, K // (2 * TILE)), 0, 2)
    mask = jnp.stack([1 - picks, picks], axis=-1)
    return mask.reshape(2, M // TILE, K // TILE).astype(jnp.int32)


def single_map(key):
    count = M // ROWS_DEV
    base = ROWS_DEV // count
    spread = base // 2
    keys = jax.random.split(key, 4)
    order = jax.random.permutation(keys[0], count)
    turns = jax.random.randint(keys[1], (count // 2,), 0, spread + 1).astype(jnp.int32)
    turns = turns.at[0].set(spread)
    amounts = jnp.zeros((count,), jnp.int32)
    amounts = amounts.at[order[0::2]].set(base + turns)
    amounts = amounts.at[order[1::2]].set(base - turns)
    offsets = jnp.repeat(jnp.arange(count, dtype=jnp.int32), amounts, total_repeat_length=ROWS_DEV)
    layers = jax.vmap(lambda inner: jax.random.permutation(inner, ROWS_DEV))(jax.random.split(keys[2], count))
    slots = jax.vmap(lambda inner: jax.random.permutation(inner, ROWS_DEV))(jax.random.split(keys[3], count))
    source = jnp.arange(count, dtype=jnp.int32)[:, None]
    target = (source + offsets[layers]) % count
    parent = target * ROWS_DEV + slots[target, layers]
    return parent.reshape(-1).astype(jnp.int32)


def draw_row_map(key, part):
    first = single_map(jax.random.fold_in(key, 11))
    second = single_map(jax.random.fold_in(key, 23))
    return jnp.stack([first, second], axis=0).astype(jnp.int32)


def block_scale(own_key, extent, pieces, smallest, largest):
    loudness, own = 1.0, jax.random.fold_in(own_key, 6)
    for dim, shards_of in pieces:
        draws = jnp.exp(jax.random.uniform(jax.random.fold_in(own, dim), (shards_of,), jnp.float32, smallest / len(pieces), largest / len(pieces)))
        loudness = loudness * jnp.repeat(draws, extent[dim] // shards_of).reshape([-1 if axis == dim else 1 for axis in range(len(extent))])
    return loudness


def normal_values(rng, shape, scale, bound, shards=(), held_as=jnp.bfloat16):
    values = scale * jax.random.normal(rng, shape, jnp.float32)
    if shards:
        values = values * block_scale(rng, shape, shards, -0.22, 0.18)
    return jnp.clip(values, -bound, bound).astype(held_as)


def setup_inputs(seed: int = 0) -> dict:
    seeds = jax.random.split(jax.random.key(seed), 7)
    schur = normal_values(seeds[0], (CHILDREN, M, W), 1.0, 6.0, ((1, 8), (2, 4)), jnp.float32)
    lower = normal_values(seeds[1], (CHILDREN, M, K), 1.0, 6.0, ((1, 8), (2, 4)))
    upper = normal_values(seeds[2], (CHILDREN, K, W), (K // 2) ** -0.5, 0.1875, ((1, 8), (2, 4)))
    tile_mask = draw_tile_mask(jax.random.fold_in(seeds[6], 71), 0)
    row_map = draw_row_map(jax.random.fold_in(seeds[6], 71), 0)
    front = normal_values(seeds[5], (M, W), 1.0, 6.0, ((0, 8), (1, 4)), jnp.float32)
    return dict(schur=schur, lower=lower, upper=upper, tile_mask=tile_mask, row_map=row_map, front=front)


def reference(schur, lower, upper, tile_mask, row_map, front):
    result = front
    for child in range(2):
        mask_full = jnp.repeat(jnp.repeat(tile_mask[child], TILE, axis=0), TILE, axis=1).astype(lower.dtype)
        masked = lower[child] * mask_full
        update = jnp.dot(masked, upper[child], preferred_element_type=jnp.float32)
        contribution = schur[child] - update
        result = result.at[row_map[child]].add(contribution)
    return result
```

```python
import jax
import jax.numpy as jnp
from jax import lax
from jax.sharding import PartitionSpec as P

TILE = 128
SCALE = 8192.0


def inner_factor(count):
    inner = 1
    while (2 * inner) * (2 * inner) <= count:
        inner *= 2
    return inner


def gather_rows(block, count):
    inner = inner_factor(count)
    outer = count // inner

    def send(x, pairs):
        return lax.ppermute(x, "row", pairs)

    def along(step, first, last):
        return [
            (z * inner + x, (z + step) * inner + x) for z in range(first, last) for x in range(inner)
        ]

    def across(step, first, last):
        return [
            (z * inner + x, z * inner + (x + step) % inner)
            for z in range(first, last)
            for x in range(inner)
        ]

    here = lax.axis_index("row") // inner
    up, down = block, block
    ups, downs = {}, {}
    for k in range(1, outer):
        up = send(up, along(1, k - 1, outer - 1))
        down = send(down, along(-1, 1, outer - k + 1))
        ups[k] = [up] + [send(up, across(j, k, outer)) for j in range(1, inner)]
        downs[k] = [down] + [send(down, across(j, 0, outer - k)) for j in range(1, inner)]
    found = [(0, j, block if j == 0 else send(block, across(j, 0, outer))) for j in range(inner)]
    for k in range(1, outer):
        for j in range(inner):
            found.append((k, j, jnp.where(here >= k, ups[k][j], downs[outer - k][j])))
    return found, inner, outer


def shards(schur, lower, upper, tile_mask, row_map, front):
    children, rows, local_depth = lower.shape
    width = schur.shape[-1]
    count = lax.axis_size("row")
    cap = 3 * rows // (2 * count)
    slots = count * cap
    row_tiles = rows // TILE
    pairs = local_depth // (2 * TILE)
    codes = 2**pairs

    blocks, inner, outer = gather_rows(upper, count)

    target = row_map // rows
    place = row_map % rows
    before = jnp.tril(jnp.ones((rows, rows), jnp.bool_), -1)
    rank = jnp.sum((target[:, :, None] == target[:, None, :]) & before[None], axis=2, dtype=jnp.int32)
    slot = target * cap + rank
    picks = tile_mask.reshape(children, row_tiles, pairs, 2)[..., 1]
    code = jnp.sum(picks * (2 ** jnp.arange(pairs, dtype=jnp.int32)), axis=-1)
    code = jnp.repeat(code, TILE, axis=1)
    row_ids = jnp.arange(rows, dtype=jnp.int32)
    tag = (code * rows + place) * rows + row_ids[None] + 1
    slot_ids = jnp.arange(slots, dtype=jnp.int32)
    tags = jnp.sum(
        jnp.where(slot[:, None, :] == slot_ids[None, :, None], tag[:, None, :], 0), axis=2, dtype=jnp.int32
    )
    source = jnp.maximum(tags - 1, 0) % rows

    tiles = lower.reshape(children, row_tiles, TILE, pairs, 2, TILE)
    second = picks.reshape(children, row_tiles, 1, pairs, 1) == 1
    compact = jnp.where(second, tiles[..., 1, :], tiles[..., 0, :]).reshape(children, rows, pairs * TILE)
    child_ids = jnp.arange(children, dtype=jnp.int32)[:, None]

    def rows_to_parents(x):
        return lax.all_to_all(
            x.reshape(x.shape[:-2] + (count, cap) + x.shape[-1:]), "row", split_axis=x.ndim - 2, concat_axis=x.ndim - 2, tiled=True
        ).reshape(x.shape)

    got_tags = lax.all_to_all(tags.reshape(children, count, cap), "row", split_axis=1, concat_axis=1, tiled=True)
    got_tags = got_tags.reshape(children, slots)
    got_lower = rows_to_parents(compact[child_ids, source])
    got_schur = []
    for child in range(children):
        sent = (schur[child][source[child]] * SCALE).astype(jnp.float16)
        got_schur.append(rows_to_parents(sent))

    got_place = jnp.where(got_tags > 0, (got_tags - 1) // rows % rows, rows)
    got_code = (got_tags - 1) // (rows * rows)
    note = slot_ids[None] * codes + got_code
    notes = jnp.sum(
        jnp.where(got_place[:, None, :] == row_ids[None, :, None], note[:, None, :], 0), axis=2, dtype=jnp.int32
    )
    where_from = notes // codes
    bits = (notes % codes)[:, :, None] // (2 ** jnp.arange(pairs, dtype=jnp.int32)) % 2
    parent_lower = got_lower[child_ids, where_from].reshape(children, rows, pairs, 1, TILE)
    halves = jnp.arange(2, dtype=jnp.int32)
    full = jnp.where(bits[..., None, None] == halves[:, None], parent_lower, 0).astype(jnp.bfloat16)
    full = lax.all_gather(full.reshape(children, rows, local_depth), "col", axis=2, tiled=True)

    me = lax.axis_index("row")
    z, x = me // inner, me % inner
    depth = upper.shape[1]
    lefts, rights = [], []
    for k, j, block in blocks:
        owner = ((z - k + outer) % outer) * inner + (x - j + inner) % inner
        for child in range(children):
            lefts.append(lax.dynamic_slice_in_dim(full[child], owner * depth, depth, axis=1))
            rights.append(block[child])
    update = jnp.dot(
        jnp.concatenate(lefts, axis=1), jnp.concatenate(rights, axis=0), preferred_element_type=jnp.float32
    )
    result = front - update
    for child in range(children):
        result = result + got_schur[child][where_from[child]].astype(jnp.float32) * (1.0 / SCALE)
    return result


def solution(mesh):
    in_specs = (
        P(None, "row", "col"),
        P(None, "row", "col"),
        P(None, "row", "col"),
        P(None, "row", "col"),
        P(None, "row"),
        P("row", "col"),
    )
    out_specs = P("row", "col")
    return jax.shard_map(shards, mesh=mesh, in_specs=in_specs, out_specs=out_specs, check_vma=False)
```

```python
import functools

import jax
import jax.numpy as jnp
from jax import lax
from jax.experimental import pallas as pl
from jax.experimental.pallas import tpu as pltpu
from jax.sharding import PartitionSpec as P

TILE = 128
LANES = 128
TOP = 32767.0
TINY = 1e-33
VMEM_LIMIT = 48 * 1024 * 1024
ANY = pl.BlockSpec(memory_space=pl.ANY)


def inner_factor(count):
    inner = 1
    while (2 * inner) * (2 * inner) <= count:
        inner *= 2
    return inner


def gate_kernel(*refs):
    pass


def gate(x, *first):
    return pl.pallas_call(
        gate_kernel,
        out_shape=jax.ShapeDtypeStruct(x.shape, x.dtype),
        in_specs=[ANY] * (1 + len(first)),
        out_specs=ANY,
        input_output_aliases={0: 0},
        name="gate",
    )(x, *first)


def pack_kernel(groups, steps, source, x, first, out, held):
    i = pl.program_id(0)
    rows = x.shape[0]
    per = 16 // groups

    @pl.when(i < steps)
    def _():
        def body(g, carry):
            at = pl.multiple_of(g * 8, 8)
            v = x[pl.ds(at, 8), :]
            most = jnp.max(jnp.abs(v), axis=1, keepdims=True)
            inverse = jnp.where(most > TINY, TOP / most, 0.0)
            q = jnp.floor(v * inverse + 0.5).astype(jnp.int32)
            base = (i * rows + at) * groups
            for j in range(groups):
                held[pl.ds(base + j, 8, stride=groups), :] = q[:, j * LANES : (j + 1) * LANES]
            return carry

        lax.fori_loop(0, rows // 8, body, 0, unroll=4)

    @pl.when(i >= steps)
    def _():
        tiles = out.shape[0]
        start = (i - steps) * tiles * per

        def body(t, carry):
            parts = []
            for a in range(per):
                row = pl.multiple_of(source[start + t * per + a] * groups, groups)
                parts.append(held[pl.ds(row, groups), :])
            out[t] = jnp.concatenate(parts, axis=0).astype(jnp.int16)
            return carry

        lax.fori_loop(0, tiles, body, 0, unroll=8)


def pack(x, source, first):
    rows, width = x.shape
    slots = source.shape[0]
    groups = width // LANES
    per = 16 // groups
    steps, out_steps = 4, 8
    tiles = slots // per // out_steps
    return pl.pallas_call(
        functools.partial(pack_kernel, groups, steps),
        out_shape=jax.ShapeDtypeStruct((slots // per, 16, LANES), jnp.int16),
        grid_spec=pltpu.PrefetchScalarGridSpec(
            num_scalar_prefetch=1,
            grid=(steps + out_steps,),
            in_specs=[
                pl.BlockSpec((rows // steps, width), lambda i, s: (jnp.minimum(i, steps - 1), 0)),
                ANY,
            ],
            out_specs=pl.BlockSpec((tiles, 16, LANES), lambda i, s: (jnp.maximum(i - steps, 0), 0, 0)),
            scratch_shapes=[pltpu.VMEM((rows * groups, LANES), jnp.int32)],
        ),
        compiler_params=pltpu.CompilerParams(vmem_limit_bytes=VMEM_LIMIT),
        cost_estimate=pl.CostEstimate(flops=8 * rows * width, bytes_accessed=7 * rows * width, transcendentals=0),
        name="pack",
    )(source, x, first)


def unpack_kernel(groups, steps, place, scale, got, before, out, held):
    i = pl.program_id(0)
    per = 16 // groups

    @pl.when(i < steps)
    def _():
        tiles = got.shape[0]
        start = i * tiles * per

        def body(t, carry):
            v = got[t].astype(jnp.int32).astype(jnp.float32)
            for a in range(per):
                s = start + t * per + a
                row = pl.multiple_of(place[s] * groups, groups)
                held[pl.ds(row, groups), :] = v[a * groups : (a + 1) * groups] * scale[s]
            return carry

        lax.fori_loop(0, tiles, body, 0, unroll=8)

    @pl.when(i >= steps)
    def _():
        rows = out.shape[0]

        def body(g, carry):
            at = pl.multiple_of(g * 8, 8)
            base = ((i - steps) * rows + at) * groups
            for j in range(groups):
                piece = held[pl.ds(base + j, 8, stride=groups), :]
                cols = pl.ds(j * LANES, LANES)
                out[pl.ds(at, 8), cols] = before[pl.ds(at, 8), cols] + piece
            return carry

        lax.fori_loop(0, rows // 8, body, 0, unroll=4)


def unpack(got, place, scale, before):
    rows, width = before.shape
    slots = place.shape[0]
    groups = width // LANES
    per = 16 // groups
    steps, out_steps = 8, 4
    tiles = slots // per // steps
    return pl.pallas_call(
        functools.partial(unpack_kernel, groups, steps),
        out_shape=jax.ShapeDtypeStruct((rows, width), jnp.float32),
        grid_spec=pltpu.PrefetchScalarGridSpec(
            num_scalar_prefetch=2,
            grid=(steps + out_steps,),
            in_specs=[
                pl.BlockSpec((tiles, 16, LANES), lambda i, p, s: (jnp.minimum(i, steps - 1), 0, 0)),
                pl.BlockSpec((rows // out_steps, width), lambda i, p, s: (jnp.maximum(i - steps, 0), 0)),
            ],
            out_specs=pl.BlockSpec((rows // out_steps, width), lambda i, p, s: (jnp.maximum(i - steps, 0), 0)),
            scratch_shapes=[pltpu.VMEM(((rows + 8) * groups, LANES), jnp.float32)],
        ),
        compiler_params=pltpu.CompilerParams(vmem_limit_bytes=VMEM_LIMIT),
        cost_estimate=pl.CostEstimate(flops=4 * rows * width, bytes_accessed=11 * rows * width, transcendentals=0),
        name="unpack",
    )(place, scale, got, before)


def lower_pack_kernel(picks, low, slot, out, compact):
    c = pl.program_id(0)
    rows, wide = compact.shape
    pairs = wide // TILE
    for i in range(rows // TILE):
        for j in range(pairs):
            column = (2 * j + picks[(c * (rows // TILE) + i) * pairs + j]) * TILE
            at = pl.ds(i * TILE, TILE)
            compact[at, j * TILE : (j + 1) * TILE] = low[0, at, pl.ds(pl.multiple_of(column, TILE), TILE)]
    step = 256

    def body(t, carry):
        at = pl.multiple_of(t * step, step)
        ids = lax.broadcasted_iota(jnp.int32, (step, rows), 0) + at
        hit = jnp.where(slot[0] == ids, 1.0, 0.0).astype(jnp.bfloat16)
        out[0, pl.ds(at, step), :] = jnp.dot(
            hit, compact[...], preferred_element_type=jnp.float32
        ).astype(jnp.bfloat16)
        return carry

    lax.fori_loop(0, out.shape[1] // step, body, 0)


def lower_pack(lower, picks, slot, slots):
    children, rows, depth = lower.shape
    wide = depth // 2
    return pl.pallas_call(
        lower_pack_kernel,
        out_shape=jax.ShapeDtypeStruct((children, slots, wide), jnp.bfloat16),
        grid_spec=pltpu.PrefetchScalarGridSpec(
            num_scalar_prefetch=1,
            grid=(children,),
            in_specs=[
                pl.BlockSpec((1, rows, depth), lambda c, p: (c, 0, 0)),
                pl.BlockSpec((1, 1, rows), lambda c, p: (c, 0, 0)),
            ],
            out_specs=pl.BlockSpec((1, slots, wide), lambda c, p: (c, 0, 0)),
            scratch_shapes=[pltpu.VMEM((rows, wide), jnp.bfloat16)],
        ),
        compiler_params=pltpu.CompilerParams(vmem_limit_bytes=VMEM_LIMIT),
        name="lower_pack",
    )(picks.reshape(-1), lower, slot.reshape(children, 1, rows))


def lower_unpack_kernel(got, place, code, out):
    slots, wide = got.shape[1:]
    rows = out.shape[1]
    step = 256

    def body(t, carry):
        at = pl.multiple_of(t * step, step)
        ids = lax.broadcasted_iota(jnp.int32, (step, slots), 0) + at
        hit = place[0] == ids
        mine = jnp.dot(
            jnp.where(hit, 1.0, 0.0).astype(jnp.bfloat16), got[0], preferred_element_type=jnp.float32
        )
        bits = jnp.sum(jnp.where(hit, code[0], 0.0), axis=1, keepdims=True).astype(jnp.int32)
        for j in range(wide // TILE):
            bit = (bits >> j) & 1
            for s in range(2):
                tile = jnp.where(bit == s, mine[:, j * TILE : (j + 1) * TILE], 0.0)
                out[0, pl.ds(at, step), (2 * j + s) * TILE : (2 * j + s + 1) * TILE] = tile.astype(jnp.bfloat16)
        return carry

    lax.fori_loop(0, rows // step, body, 0)


def lower_unpack(got, place, code, rows):
    children, slots, wide = got.shape
    lane = pl.BlockSpec((1, 1, slots), lambda c: (c, 0, 0))
    return pl.pallas_call(
        lower_unpack_kernel,
        out_shape=jax.ShapeDtypeStruct((children, rows, 2 * wide), jnp.bfloat16),
        grid=(children,),
        in_specs=[pl.BlockSpec((1, slots, wide), lambda c: (c, 0, 0)), lane, lane],
        out_specs=pl.BlockSpec((1, rows, 2 * wide), lambda c: (c, 0, 0)),
        compiler_params=pltpu.CompilerParams(vmem_limit_bytes=VMEM_LIMIT),
        name="lower_unpack",
    )(got, place.reshape(children, 1, slots), code.reshape(children, 1, slots))


class Relay:
    def __init__(self, block, count):
        self.inner = inner_factor(count)
        self.outer = count // self.inner
        self.up = self.down = block
        self.ups, self.downs = {}, {}
        self.own = [block] + self.exchange(block, 0, self.outer)
        self.k = 0

    def send(self, x, pairs):
        return lax.ppermute(x, "row", pairs)

    def along(self, step, first, last):
        n = self.inner
        return [(z * n + x, (z + step) * n + x) for z in range(first, last) for x in range(n)]

    def exchange(self, x, first, last):
        n = self.inner
        return [
            self.send(x, [(z * n + i, z * n + (i + j) % n) for z in range(first, last) for i in range(n)])
            for j in range(1, n)
        ]

    def step(self):
        if self.k + 1 >= self.outer:
            return
        self.k += 1
        self.up = self.send(self.up, self.along(1, self.k - 1, self.outer - 1))
        self.down = self.send(self.down, self.along(-1, 1, self.outer - self.k + 1))
        self.ups[self.k] = [self.up] + self.exchange(self.up, self.k, self.outer)
        self.downs[self.k] = [self.down] + self.exchange(self.down, 0, self.outer - self.k)

    def blocks(self):
        while self.k + 1 < self.outer:
            self.step()
        me = lax.axis_index("row")
        z, x = me // self.inner, me % self.inner
        found = []
        for k in range(self.outer):
            for j in range(self.inner):
                block = self.own[j] if k == 0 else jnp.where(z >= k, self.ups[k][j], self.downs[self.outer - k][j])
                owner = ((z - k + self.outer) % self.outer) * self.inner + (x - j + self.inner) % self.inner
                found.append((owner, block))
        return found


def shards(schur, lower, upper, tile_mask, row_map, front):
    children, rows, local_depth = lower.shape
    count = lax.axis_size("row")
    me = lax.axis_index("row")
    cap = 3 * rows // (2 * count)
    slots = count * cap
    row_tiles = rows // TILE
    pairs = local_depth // (2 * TILE)

    relay = Relay(upper, count)
    relay.step()

    target = row_map // rows
    place = row_map % rows
    earlier = jnp.tril(jnp.ones((rows, rows), jnp.bool_), -1)
    rank = jnp.sum((target[:, :, None] == target[:, None, :]) & earlier[None], axis=2, dtype=jnp.int32)
    slot = target * cap + rank
    picks = tile_mask.reshape(children, row_tiles, pairs, 2)[..., 1]
    code = jnp.sum(picks * (2 ** jnp.arange(pairs, dtype=jnp.int32)), axis=-1)
    tag = (jnp.repeat(code, TILE, axis=1) * rows + place + 1).astype(jnp.float32)
    slot_ids = jnp.arange(slots, dtype=jnp.int32)
    row_ids = jnp.arange(rows, dtype=jnp.int32)
    goes = slot[:, None, :] == slot_ids[None, :, None]
    source = jnp.sum(jnp.where(goes, row_ids, 0), axis=2, dtype=jnp.int32)
    tags = jnp.sum(jnp.where(goes, tag[:, None, :], 0.0), axis=2)
    scale = jnp.max(jnp.abs(schur), axis=2) * (1.0 / TOP)
    scales = jnp.sum(jnp.where(goes, scale[:, None, :], 0.0), axis=2)
    notes = lax.all_gather(jnp.stack([tags, scales]), "row", axis=0)
    notes = lax.dynamic_slice_in_dim(notes, me * cap, cap, axis=3)
    notes = notes.transpose(1, 2, 0, 3).reshape(2, children, slots)
    got_tags = notes[0].astype(jnp.int32)
    got_place = jnp.where(got_tags > 0, (got_tags - 1) % rows, rows)
    got_code = ((got_tags - 1) // rows).astype(jnp.float32)
    got_scale = notes[1]

    def to_parents(x, per_slot):
        shape = (count, x.shape[0] // count) + x.shape[1:]
        return lax.all_to_all(x.reshape(shape), "row", split_axis=0, concat_axis=0, tiled=True).reshape(x.shape)

    sent_lower = lower_pack(lower, picks, slot, slots)
    got_lower = lax.all_to_all(
        sent_lower.reshape(children, count, cap, -1), "row", split_axis=1, concat_axis=1, tiled=True
    ).reshape(sent_lower.shape)
    sent = [pack(schur[0], source[0], sent_lower)]
    sent.append(pack(schur[1], source[1], sent[0]))
    got = [to_parents(gate(sent[0], got_lower, relay.up, relay.down), 1)]
    relay.step()
    got.append(to_parents(gate(sent[1], got[0], relay.up, relay.down), 1))

    full = lower_unpack(got_lower, got_place, got_code, rows)
    full = lax.all_gather(full, "col", axis=2, tiled=True)
    depth = upper.shape[1]
    lefts, rights = [], []
    for owner, block in relay.blocks():
        for child in range(children):
            lefts.append(lax.dynamic_slice_in_dim(full[child], owner * depth, depth, axis=1))
            rights.append(block[child])
    result = front - jnp.dot(
        jnp.concatenate(lefts, axis=1), jnp.concatenate(rights, axis=0), preferred_element_type=jnp.float32
    )
    for child in range(children):
        result = unpack(got[child], got_place[child], got_scale[child], result)
    return result


def solution(mesh):
    in_specs = (
        P(None, "row", "col"),
        P(None, "row", "col"),
        P(None, "row", "col"),
        P(None, "row", "col"),
        P(None, "row"),
        P("row", "col"),
    )
    out_specs = P("row", "col")
    return jax.shard_map(shards, mesh=mesh, in_specs=in_specs, out_specs=out_specs, check_vma=False)
```

```python
import functools
import math

import jax
import jax.numpy as jnp
from jax import lax
from jax.experimental import pallas as pl
from jax.experimental.pallas import tpu as pltpu
from jax.sharding import PartitionSpec as P

TILE = 128
LANES = 128
TOP = 32767.0
FINE = 256
LEAST = 1e-30
VMEM_LIMIT = 56 * 1024 * 1024
ANY = pl.BlockSpec(memory_space=pl.ANY)


def inner_factor(count):
    inner = 1
    while (2 * inner) * (2 * inner) <= count:
        inner *= 2
    return inner


def takes(us):
    return pl.CostEstimate(flops=int(us * 4e9), bytes_accessed=int(us * 3.3e6), transcendentals=0)


def gate_kernel(*refs):
    pass


def gate(arrays, *first):
    count = len(arrays)
    return pl.pallas_call(
        gate_kernel,
        out_shape=[jax.ShapeDtypeStruct(x.shape, x.dtype) for x in arrays],
        in_specs=[ANY] * (count + len(first)),
        out_specs=[ANY] * count,
        input_output_aliases={i: i for i in range(count)},
        name="gate",
    )(*arrays, *first)


def unit_of(code):
    return jnp.exp(code * (math.log(2.0) / FINE))


def mask_kernel(mask, low, out):
    c = pl.program_id(0)
    _, rows, depth = low.shape
    row_tiles, tiles = rows // TILE, depth // TILE
    for i in range(row_tiles):
        for j in range(tiles):
            at = (0, slice(i * TILE, (i + 1) * TILE), slice(j * TILE, (j + 1) * TILE))
            keep = mask[(c * row_tiles + i) * tiles + j] != 0

            @pl.when(keep)
            def _():
                out[at] = low[at]

            @pl.when(jnp.logical_not(keep))
            def _():
                out[at] = jnp.zeros((TILE, TILE), out.dtype)


def mask_tiles(lower, mask):
    children, rows, depth = lower.shape
    block = pl.BlockSpec((1, rows, depth), lambda c, m: (c, 0, 0))
    return pl.pallas_call(
        mask_kernel,
        out_shape=jax.ShapeDtypeStruct(lower.shape, lower.dtype),
        grid_spec=pltpu.PrefetchScalarGridSpec(
            num_scalar_prefetch=1, grid=(children,), in_specs=[block], out_specs=block
        ),
        compiler_params=pltpu.CompilerParams(vmem_limit_bytes=VMEM_LIMIT),
        cost_estimate=takes(4),
        name="mask_tiles",
    )(mask.reshape(-1), lower)


def send_kernel(groups, steps, parts, blocks, source, starts, slot, notes, schur, *refs):
    lows, ups = refs[:parts], refs[parts : parts + blocks]
    out, low_all, up_all, total, scale, held, codes, sems = refs[parts + blocks :]
    i = pl.program_id(0)
    rows, width = schur.shape[1:]
    targets, tiles = out.shape[0], out.shape[1] - 1
    per = 16 // groups
    stride = codes.shape[1] // (targets * (pl.num_programs(0) - steps))

    @pl.when(i == 0)
    def _():
        copies = []
        for n, low in enumerate(lows):
            at = pl.ds(pl.multiple_of(starts[n], low.shape[1]), low.shape[1])
            copies.append(pltpu.make_async_copy(low, low_all.at[:, at], sems.at[n]))
        for n, up in enumerate(ups):
            at = pl.ds(pl.multiple_of(starts[parts + n], up.shape[0]), up.shape[0])
            copies.append(pltpu.make_async_copy(up, up_all.at[at], sems.at[parts + n]))
        for copy in copies:
            copy.start()
        codes[...] = jnp.zeros(codes.shape, jnp.float32)
        for copy in copies:
            copy.wait()

    @pl.when(i < steps)
    def _():
        here = pl.ds(pl.multiple_of(i * rows, rows), rows)
        total[...] = schur[0] - jnp.dot(low_all[here, :], up_all[...], preferred_element_type=jnp.float32)
        most = jnp.maximum(jnp.max(jnp.abs(total[...]), axis=1, keepdims=True), LEAST)
        code = jnp.floor(jnp.log(most) * (FINE / math.log(2.0)) - FINE * math.log2(TOP)) + 2.0
        scale[0] = jnp.broadcast_to(1.0 / unit_of(code), (rows, LANES))
        scale[1] = jnp.broadcast_to(code, (rows, LANES))

        def body(g, carry):
            at = pl.multiple_of(g * 8, 8)
            inverse = scale[0, pl.ds(at, 8), :]
            base = (i * rows + at) * groups
            for j in range(groups):
                v = total[pl.ds(at, 8), j * LANES : (j + 1) * LANES]
                held[pl.ds(base + j, 8, stride=groups), :] = jnp.floor(v * inverse + 0.5).astype(jnp.int32)
            return carry

        lax.fori_loop(0, rows // 8, body, 0, unroll=4)

        for lane in range(0, codes.shape[1], 8 * LANES):
            lanes = lax.broadcasted_iota(jnp.int32, (8, 8 * LANES), 1) + lane

            def note(g, carry):
                at = pl.multiple_of(g * 8, 8)
                mine = jnp.concatenate([scale[1, pl.ds(at, 8), :]] * 8, axis=1)
                place = jnp.concatenate([slot[pl.ds(at, 8), :]] * 8, axis=1)
                return carry + jnp.where(place == lanes, mine, 0.0)

            codes[:, lane : lane + 8 * LANES] += lax.fori_loop(
                0, rows // 8, note, jnp.zeros(lanes.shape, jnp.float32), unroll=4
            )

    @pl.when(i >= steps)
    def _():
        for target in range(targets):
            number = (i - steps) * targets + target
            start = number * tiles * per

            def body(t, carry):
                pieces = []
                for a in range(per):
                    row = pl.multiple_of(source[start + t * per + a], groups)
                    pieces.append(held[pl.ds(row, groups), :])
                out[target, t] = jnp.concatenate(pieces, axis=0).astype(jnp.int16)
                return carry

            lax.fori_loop(0, tiles, body, 0, unroll=8)
            tile = notes[target]
            line = lax.broadcasted_iota(jnp.int32, tile.shape, 0)
            mine = jnp.sum(codes[:, pl.ds(pl.multiple_of(number * stride, stride), stride)], axis=0, keepdims=True)
            for a in range(stride // LANES):
                piece = mine[:, a * LANES : (a + 1) * LANES].astype(jnp.int32)
                tile = jnp.where(line == stride // LANES + a, piece, tile)
            out[target, tiles] = tile.astype(jnp.int16)


def send_rows(child, schur, lows, ups, starts, source, slot, notes):
    rows, width = schur.shape[1:]
    count = notes.shape[0]
    cap = source.shape[0] // count
    groups = width // LANES
    tiles = cap * groups // 16
    steps, out_steps = 2, 2
    depth = sum(up.shape[0] for up in ups)
    stride = -(-cap // LANES) * LANES
    first = lambda i, *_: jnp.minimum(i, steps - 1)
    second = lambda i, *_: jnp.maximum(i - steps, 0)
    return pl.pallas_call(
        functools.partial(send_kernel, groups, steps, len(lows), len(ups)),
        out_shape=jax.ShapeDtypeStruct((count, tiles + 1, 16, LANES), jnp.int16),
        grid_spec=pltpu.PrefetchScalarGridSpec(
            num_scalar_prefetch=2,
            grid=(steps + out_steps,),
            in_specs=[
                pl.BlockSpec((rows // steps, LANES), lambda i, *_: (first(i), 0)),
                pl.BlockSpec((count // out_steps, 16, LANES), lambda i, *_: (second(i), 0, 0)),
                pl.BlockSpec((1, rows // steps, width), lambda i, *_: (child, first(i), 0)),
            ]
            + [ANY] * (len(lows) + len(ups)),
            out_specs=pl.BlockSpec((count // out_steps, tiles + 1, 16, LANES), lambda i, *_: (second(i), 0, 0, 0)),
            scratch_shapes=[
                pltpu.VMEM((rows, depth), jnp.bfloat16),
                pltpu.VMEM((depth, width), jnp.bfloat16),
                pltpu.VMEM((rows // steps, width), jnp.float32),
                pltpu.VMEM((2, rows // steps, LANES), jnp.float32),
                pltpu.VMEM((rows * groups, LANES), jnp.int32),
                pltpu.VMEM((8, count * stride), jnp.float32),
                pltpu.SemaphoreType.DMA((len(lows) + len(ups),)),
            ],
        ),
        compiler_params=pltpu.CompilerParams(vmem_limit_bytes=VMEM_LIMIT),
        cost_estimate=takes(14),
        name="send_rows",
    )(source * groups, starts, slot, notes, schur, *lows, *ups)


def receive_kernel(groups, steps, cap, got, notes, before, out, held, plain, size, scale, place, sem):
    i = pl.program_id(0)
    count = notes.shape[0]
    per = 16 // groups
    chunk = 16
    lines = -(-cap // LANES)

    @pl.when(i == 0)
    def _():
        for s in range(count):
            note = notes[s, 0].astype(jnp.int32)
            plain[s * (lines + 1) : (s + 1) * (lines + 1), :] = jnp.concatenate(
                [note[:lines] * groups, note[2 * lines : 2 * lines + 1]], axis=0
            )
            size[s * lines : (s + 1) * lines, :] = unit_of(note[lines : 2 * lines].astype(jnp.float32))
        copy = pltpu.make_async_copy(plain, place, sem)
        copy.start()
        copy.wait()

    def collect(device, s):
        def body(k, carry):
            line = device * (lines + 1) + k // (LANES // chunk)
            lane = k % (LANES // chunk) * chunk
            for t in range(chunk // per):
                v = got[s, k * (chunk // per) + t].astype(jnp.int32).astype(jnp.float32)
                for a in range(per):
                    row = pl.multiple_of(place[line, lane + t * per + a], groups)
                    held[pl.ds(row, groups), :] = v[a * groups : (a + 1) * groups]
            return carry

        lax.fori_loop(0, (place[device * (lines + 1) + lines, 0] + chunk - 1) // chunk, body, 0)

    @pl.when(i < steps)
    def _():
        for s in range(count // steps):
            collect(i * (count // steps) + s, s)

    @pl.when(i >= steps)
    def _():
        rows = out.shape[0]
        start = (i - steps) * rows
        ids = (lax.broadcasted_iota(jnp.int32, (rows, LANES), 0) + start + 1) * groups

        def find(s, carry):
            for a in range(lines):
                here = plain[pl.ds(s * (lines + 1) + a, 1), :] == ids
                carry += jnp.where(here, size[pl.ds(s * lines + a, 1), :], 0.0)
            return carry

        unit = lax.fori_loop(0, count, find, jnp.zeros(ids.shape, jnp.float32))
        scale[...] = jnp.broadcast_to(jnp.sum(unit, axis=1, keepdims=True), scale.shape)

        def body(g, carry):
            at = pl.multiple_of(g * 8, 8)
            unit = scale[pl.ds(at, 8), :]
            for j in range(groups):
                cols = pl.ds(j * LANES, LANES)
                piece = held[pl.ds((start + at + 1) * groups + j, 8, stride=groups), :]
                out[pl.ds(at, 8), cols] = before[pl.ds(at, 8), cols] + piece * unit
            return carry

        lax.fori_loop(0, rows // 8, body, 0, unroll=4)


def receive_rows(got, cap, before):
    rows, width = before.shape
    count, tiles = got.shape[0], got.shape[1] - 1
    groups = width // LANES
    lines = -(-cap // LANES)
    steps, out_steps = count // 2, 2
    block = pl.BlockSpec((rows // out_steps, width), lambda i: (jnp.maximum(i - steps, 0), 0))
    return pl.pallas_call(
        functools.partial(receive_kernel, groups, steps, cap),
        out_shape=jax.ShapeDtypeStruct((rows, width), jnp.float32),
        grid=(steps + out_steps,),
        in_specs=[
            pl.BlockSpec((count // steps, tiles, 16, LANES), lambda i: (jnp.minimum(i, steps - 1), 0, 0, 0)),
            pl.BlockSpec((count, 1, 16, LANES), lambda i: (0, tiles, 0, 0)),
            block,
        ],
        out_specs=block,
        scratch_shapes=[
            pltpu.VMEM(((rows + 1) * groups, LANES), jnp.float32),
            pltpu.VMEM((count * (lines + 1), LANES), jnp.int32),
            pltpu.VMEM((count * lines, LANES), jnp.float32),
            pltpu.VMEM((rows // out_steps, LANES), jnp.float32),
            pltpu.SMEM((count * (lines + 1), LANES), jnp.int32),
            pltpu.SemaphoreType.DMA,
        ],
        compiler_params=pltpu.CompilerParams(vmem_limit_bytes=VMEM_LIMIT),
        cost_estimate=takes(8),
        name="receive_rows",
    )(got, got, before)


class Relay:
    def __init__(self, block, count):
        self.inner = inner_factor(count)
        self.outer = count // self.inner
        self.z = lax.axis_index("row") // self.inner
        self.x = lax.axis_index("row") % self.inner
        self.up = self.down = block
        self.came = {}
        self.order = [
            [(k, d) for k in range(1, self.outer) for d in (1, -1) if 0 <= z - d * k < self.outer]
            for z in range(self.outer)
        ]
        self.held = [[block] + self.exchange(block, range(self.outer))]
        self.k = 0

    def send(self, x, moves, turn=0):
        n = self.inner
        return lax.ppermute(
            x, "row", [(z * n + i, to * n + (i + turn) % n) for z, to in moves.items() for i in range(n)]
        )

    def exchange(self, x, where):
        return [self.send(x, {z: z for z in where}, j) for j in range(1, self.inner)]

    def choose(self, number, where):
        names = {z: self.order[z][number - 1] for z in where}
        every = sorted(set(names.values()))
        block = self.came[every[0]]
        for name in every[1:]:
            here = functools.reduce(jnp.logical_or, [self.z == z for z in where if names[z] == name])
            block = jnp.where(here, self.came[name], block)
        return block

    def step(self):
        if self.k:
            block = self.choose(self.k, range(self.outer))
            self.held.append([block] + self.exchange(block, range(self.outer)))
        self.k += 1
        last = self.outer - 1
        if self.k == last:
            inside = range(1, last)
            block = self.choose(last, inside)
            ends = {1: 0, last - 1: last}
            at_end = (self.z == 0) | (self.z == last)
            others = [block] + self.exchange(block, inside)
            self.held.append(
                [jnp.where(at_end, self.send(block, ends, j), others[j]) for j in range(self.inner)]
            )
            return
        self.up = self.send(self.up, {z: z + 1 for z in range(self.k - 1, last)})
        self.down = self.send(self.down, {z: z - 1 for z in range(1, last - self.k + 2)})
        self.came[self.k, 1], self.came[self.k, -1] = self.up, self.down

    def pass_gate(self, arrays):
        mine = self.held[self.k - 1][1:]
        count = len(mine)
        self.up, self.down, *rest = gate([self.up, self.down, *mine, *arrays])
        self.came[self.k, 1], self.came[self.k, -1] = self.up, self.down
        self.held[self.k - 1][1:] = rest[:count]
        return rest[count:]

    def blocks(self):
        while self.k < self.outer - 1:
            self.step()
        found = []
        for k in range(self.outer):
            at = self.z
            if k:
                at = jnp.array([z - d * far for z, (far, d) in enumerate(o[k - 1] for o in self.order)], jnp.int32)[at]
            for j in range(self.inner):
                found.append((at * self.inner + (self.x - j + self.inner) % self.inner, self.held[k][j]))
        return found


def gather_columns(x):
    size = lax.axis_size("col")
    found = [(0, x)]
    bit = size // 2
    while bit:
        pairs = [(i, i ^ bit) for i in range(size)]
        found += [(far ^ bit, lax.ppermute(y, "col", pairs)) for far, y in found]
        bit //= 2
    return found


def shards(schur, lower, upper, tile_mask, row_map, front):
    children, rows, local_depth = lower.shape
    count = lax.axis_size("row")
    cap = 3 * rows // (2 * count)
    lines = -(-cap // LANES)
    stride = lines * LANES
    depth = upper.shape[1]

    target = row_map // rows
    place = row_map % rows + 1
    earlier = jnp.tril(jnp.ones((rows, rows), jnp.bool_), -1)
    same = target[:, :, None] == target[:, None, :]
    rank = jnp.sum(same & earlier[None], axis=2, dtype=jnp.int32)
    slot = target * stride + rank
    slot_ids = jnp.arange(count * stride, dtype=jnp.int32)
    goes = slot[:, None, :] == slot_ids[None, :, None]
    row_ids = jnp.arange(rows, dtype=jnp.int32)
    source = jnp.sum(jnp.where(goes, row_ids, 0), axis=2, dtype=jnp.int32)
    source = source.reshape(children, count, stride)[:, :, :cap].reshape(children, -1)
    places = jnp.sum(jnp.where(goes, place[:, None, :], 0), axis=2, dtype=jnp.int32)
    places = places.reshape(children, count, lines, LANES)
    amount = jnp.sum(places > 0, axis=(2, 3), keepdims=True, dtype=jnp.int32)
    amount = jnp.broadcast_to(amount, (children, count, 16 - 2 * lines, LANES))
    notes = jnp.concatenate([places, jnp.zeros_like(places), amount], axis=2)

    masked = mask_tiles(lower, tile_mask)
    column = lax.axis_index("col")
    relays = []
    result = front
    got = []
    for child in range(children):
        block = upper[child]
        if relays:
            (block,) = gate([block], relays[-1].up, relays[-1].down)
        relay = Relay(block, count)
        relays.append(relay)
        relay.step()
        parts = gather_columns(masked[child])
        blocks = relay.blocks()
        starts = [(column ^ far) * local_depth for far, _ in parts] + [owner * depth for owner, _ in blocks]
        sent = send_rows(
            child,
            schur,
            [part for _, part in parts],
            [block for _, block in blocks],
            jnp.stack(starts).astype(jnp.int32),
            source[child],
            jnp.broadcast_to(slot[child][:, None], (rows, LANES)),
            notes[child],
        )
        if got:
            (sent,) = gate([sent], got[-1])
        got.append(lax.all_to_all(sent, "row", split_axis=0, concat_axis=0, tiled=True))
    for child in range(children):
        result = receive_rows(got[child], cap, result)
    return result


def solution(mesh):
    in_specs = (
        P(None, "row", "col"),
        P(None, "row", "col"),
        P(None, "row", "col"),
        P(None, "row", "col"),
        P(None, "row"),
        P("row", "col"),
    )
    out_specs = P("row", "col")
    return jax.shard_map(shards, mesh=mesh, in_specs=in_specs, out_specs=out_specs, check_vma=False)
```

```python
import functools

import jax
import jax.numpy as jnp
from jax import lax
from jax.experimental import pallas as pl
from jax.experimental.pallas import tpu as pltpu
from jax.sharding import PartitionSpec as P

TILE = 128
LANES = 128
TOP = 32767.0
STEP = (1.0 + 2.0**-7) / TOP
NOTES = 16
BASE = 32
TINY = 1e-33
VMEM_LIMIT = 56 * 1024 * 1024
ANY = pl.BlockSpec(memory_space=pl.ANY)


def inner_factor(count):
    inner = 1
    while (2 * inner) * (2 * inner) <= count:
        inner *= 2
    return inner


def takes(us):
    return pl.CostEstimate(flops=int(us * 4e9), bytes_accessed=int(us * 3.3e6), transcendentals=0)


def gate_kernel(*refs):
    pass


def gate(arrays, *first):
    count = len(arrays)
    return pl.pallas_call(
        gate_kernel,
        out_shape=[jax.ShapeDtypeStruct(x.shape, x.dtype) for x in arrays],
        in_specs=[ANY] * (count + len(first)),
        out_specs=[ANY] * count,
        input_output_aliases={i: i for i in range(count)},
        name="gate",
    )(*arrays, *first)


def row_unit(x):
    most = jnp.max(jnp.abs(x), axis=-1, keepdims=True)
    return jnp.where(most > TINY, most * STEP, 0.0).astype(jnp.bfloat16)


def pack_kernel(groups, steps, source, x, *refs):
    out, held = refs[-2:]
    i = pl.program_id(0)
    rows = x.shape[1]
    targets, _, tiles = out.shape[:3]
    per = 16 // groups

    @pl.when(i < steps)
    def _():
        def body(g, carry):
            at = pl.multiple_of(g * 8, 8)
            v = x[0, pl.ds(at, 8), :]
            unit = row_unit(v).astype(jnp.float32)
            inverse = jnp.where(unit > 0.0, 1.0 / unit, 0.0)
            q = jnp.floor(v * inverse + 0.5).astype(jnp.int32)
            base = (i * rows + at) * groups
            for j in range(groups):
                held[pl.ds(base + j, 8, stride=groups), :] = q[:, j * LANES : (j + 1) * LANES]
            return carry

        lax.fori_loop(0, rows // 8, body, 0, unroll=4)

    @pl.when(i >= steps)
    def _():
        for target in range(targets):
            start = ((i - steps) * targets + target) * tiles * per

            def body(t, carry):
                parts = []
                for a in range(per):
                    row = pl.multiple_of(source[start + t * per + a] * groups, groups)
                    parts.append(held[pl.ds(row, groups), :])
                out[target, 0, t] = jnp.concatenate(parts, axis=0).astype(jnp.int16)
                return carry

            lax.fori_loop(0, tiles, body, 0, unroll=8)


def pack(x, child, source, count, into, *first):
    children, rows, width = x.shape
    cap = source.shape[0] // count
    groups = width // LANES
    tiles = cap * groups // 16
    steps, out_steps = 2, 4
    first = first if into is None else (into,) + first
    return pl.pallas_call(
        functools.partial(pack_kernel, groups, steps),
        out_shape=jax.ShapeDtypeStruct((count, children, tiles, 16, LANES), jnp.int16),
        grid_spec=pltpu.PrefetchScalarGridSpec(
            num_scalar_prefetch=1,
            grid=(steps + out_steps,),
            in_specs=[pl.BlockSpec((1, rows // steps, width), lambda i, s: (child, jnp.minimum(i, steps - 1), 0))]
            + [ANY] * len(first),
            out_specs=pl.BlockSpec(
                (count // out_steps, 1, tiles, 16, LANES),
                lambda i, s: (jnp.maximum(i - steps, 0), child, 0, 0, 0),
            ),
            scratch_shapes=[pltpu.VMEM((rows * groups, LANES), jnp.int32)],
        ),
        input_output_aliases={} if into is None else {2: 0},
        compiler_params=pltpu.CompilerParams(vmem_limit_bytes=VMEM_LIMIT),
        cost_estimate=takes(10),
        name="pack",
    )(source, x, *first)


def unpack_kernel(groups, parts, row_at, valid, got, before, unit, out, held):
    i = pl.program_id(0)
    children = unit.shape[0]
    per = 16 // groups
    chunk = 16
    tiles = got.shape[2]

    @pl.when(i < parts)
    def _():
        for c in range(children):
            base = (c * parts + i) * tiles * per

            def body(k, carry):
                for t in range(chunk // per):
                    v = got[0, c, k * (chunk // per) + t].astype(jnp.int32).astype(jnp.float32)
                    for a in range(per):
                        row = pl.multiple_of(row_at[base + k * chunk + t * per + a], groups)
                        held[c, pl.ds(row, groups), :] = v[a * groups : (a + 1) * groups]
                return carry

            lax.fori_loop(0, (valid[c * parts + i] + chunk - 1) // chunk, body, 0)

    @pl.when(i >= parts)
    def _():
        rows = out.shape[0]

        def body(g, carry):
            at = pl.multiple_of(g * 8, 8)
            base = ((i - parts) * rows + at) * groups
            for j in range(groups):
                cols = pl.ds(j * LANES, LANES)
                total = before[pl.ds(at, 8), cols]
                for c in range(children):
                    total += held[c, pl.ds(base + j, 8, stride=groups), :] * unit[c, pl.ds(at, 8), :]
                out[pl.ds(at, 8), cols] = total
            return carry

        lax.fori_loop(0, rows // 8, body, 0, unroll=2)


def unpack(got, place, unit, before):
    rows, width = before.shape
    count, children, tiles = got.shape[:3]
    groups = width // LANES
    out_steps = 4

    def block(i, *_):
        return jnp.maximum(i - count, 0), 0

    valid = jnp.sum(place < rows, axis=2, dtype=jnp.int32)
    return pl.pallas_call(
        functools.partial(unpack_kernel, groups, count),
        out_shape=jax.ShapeDtypeStruct((rows, width), jnp.float32),
        grid_spec=pltpu.PrefetchScalarGridSpec(
            num_scalar_prefetch=2,
            grid=(count + out_steps,),
            in_specs=[
                pl.BlockSpec((1, children, tiles, 16, LANES), lambda i, *_: (jnp.minimum(i, count - 1), 0, 0, 0, 0)),
                pl.BlockSpec((rows // out_steps, width), block),
                pl.BlockSpec((children, rows // out_steps, LANES), lambda i, *_: (0, block(i)[0], 0)),
            ],
            out_specs=pl.BlockSpec((rows // out_steps, width), block),
            scratch_shapes=[pltpu.VMEM((children, (rows + 8) * groups, LANES), jnp.float32)],
        ),
        compiler_params=pltpu.CompilerParams(vmem_limit_bytes=VMEM_LIMIT),
        cost_estimate=takes(11),
        name="unpack",
    )((place * groups).reshape(-1), valid.reshape(-1), got, before, unit)


def lower_pack_kernel(picks, low, slot, digits, out, compact):
    c = pl.program_id(0)
    rows, wide = compact.shape
    pairs = wide // TILE
    count, _, room, _ = out.shape
    for i in range(rows // TILE):
        for j in range(pairs):
            column = (2 * j + picks[(c * (rows // TILE) + i) * pairs + j]) * TILE
            at = pl.ds(i * TILE, TILE)
            compact[at, j * TILE : (j + 1) * TILE] = low[0, at, pl.ds(pl.multiple_of(column, TILE), TILE)]

    def body(t, carry):
        ids = lax.broadcasted_iota(jnp.int32, (max(room, wide), rows), 0) + t * room
        hit = jnp.where(slot[0] == ids, 1.0, 0.0).astype(jnp.bfloat16)
        mine = jnp.dot(hit[:room], compact[...], preferred_element_type=jnp.float32)
        out[t, 0] = mine.astype(jnp.bfloat16)
        notes = lax.dot_general(
            digits[0], hit[:wide], (((1,), (1,)), ((), ())), preferred_element_type=jnp.float32
        )
        out[t, 0, room - NOTES :, :] = notes.astype(jnp.bfloat16)
        return carry

    lax.fori_loop(0, count, body, 0)


def lower_pack(lower, picks, slot, digits, count, room):
    children, rows, depth = lower.shape
    wide = depth // 2
    return pl.pallas_call(
        lower_pack_kernel,
        out_shape=jax.ShapeDtypeStruct((count, children, room, wide), jnp.bfloat16),
        grid_spec=pltpu.PrefetchScalarGridSpec(
            num_scalar_prefetch=1,
            grid=(children,),
            in_specs=[
                pl.BlockSpec((1, rows, depth), lambda c, p: (c, 0, 0)),
                pl.BlockSpec((1, 1, rows), lambda c, p: (c, 0, 0)),
                pl.BlockSpec((1, NOTES, rows), lambda c, p: (c, 0, 0)),
            ],
            out_specs=pl.BlockSpec((count, 1, room, wide), lambda c, p: (0, c, 0, 0)),
            scratch_shapes=[pltpu.VMEM((rows, wide), jnp.bfloat16)],
        ),
        compiler_params=pltpu.CompilerParams(vmem_limit_bytes=VMEM_LIMIT),
        cost_estimate=takes(7),
        name="lower_pack",
    )(picks.reshape(-1), lower, slot.reshape(children, 1, rows), digits)


def lower_unpack_kernel(got, place, code, unit, out, units):
    count, _, room, wide = got.shape
    slots = count * room
    rows = out.shape[1]
    step = 256

    def body(t, carry):
        at = pl.multiple_of(t * step, step)
        ids = lax.broadcasted_iota(jnp.int32, (step, slots), 0) + at
        hit = place[0] == ids
        mine = jnp.dot(
            jnp.where(hit, 1.0, 0.0).astype(jnp.bfloat16),
            got[...].reshape(slots, wide),
            preferred_element_type=jnp.float32,
        )
        bits = jnp.sum(jnp.where(hit, code[0], 0.0), axis=1, keepdims=True).astype(jnp.int32)
        row = jnp.sum(jnp.where(hit, unit[0], 0.0), axis=1, keepdims=True)
        units[0, pl.ds(at, step), :] = jnp.broadcast_to(row, (step, LANES))
        for j in range(wide // TILE):
            bit = (bits >> j) & 1
            for s in range(2):
                tile = jnp.where(bit == s, mine[:, j * TILE : (j + 1) * TILE], 0.0)
                out[0, pl.ds(at, step), (2 * j + s) * TILE : (2 * j + s + 1) * TILE] = tile.astype(jnp.bfloat16)
        return carry

    lax.fori_loop(0, rows // step, body, 0)


def lower_unpack(got, rows, *lanes):
    count, children, room, wide = got.shape
    slots = count * room
    lane = pl.BlockSpec((1, 1, slots), lambda c: (c, 0, 0))
    whole = lambda n: pl.BlockSpec((1, rows, n), lambda c: (c, 0, 0))
    return pl.pallas_call(
        lower_unpack_kernel,
        out_shape=(
            jax.ShapeDtypeStruct((children, rows, 2 * wide), jnp.bfloat16),
            jax.ShapeDtypeStruct((children, rows, LANES), jnp.float32),
        ),
        grid=(children,),
        in_specs=[pl.BlockSpec((count, 1, room, wide), lambda c: (0, c, 0, 0))] + [lane] * len(lanes),
        out_specs=(whole(2 * wide), whole(LANES)),
        compiler_params=pltpu.CompilerParams(vmem_limit_bytes=VMEM_LIMIT),
        cost_estimate=takes(5),
        name="lower_unpack",
    )(got, *[x.reshape(children, 1, slots) for x in lanes])


def product_kernel(children, steps, parts, blocks, starts, front, *refs):
    lows, ups = refs[:parts], refs[parts : parts + blocks]
    out, low_all, up_all, sems = refs[parts + blocks :]
    i = pl.program_id(0)
    rows = front.shape[0]
    depth = low_all.shape[1] // children

    @pl.when(i == 0)
    def _():
        copies = []
        for c in range(children):
            for n, low in enumerate(lows):
                at = pl.ds(pl.multiple_of(c * depth + starts[n], low.shape[2]), low.shape[2])
                copies.append(pltpu.make_async_copy(low.at[c], low_all.at[:, at], sems.at[len(copies)]))
            for n, up in enumerate(ups):
                at = pl.ds(pl.multiple_of(c * depth + starts[parts + n], up.shape[1]), up.shape[1])
                copies.append(pltpu.make_async_copy(up.at[c], up_all.at[at], sems.at[len(copies)]))
        for copy in copies:
            copy.start()
        for copy in copies:
            copy.wait()

    here = pl.ds(pl.multiple_of(i * rows, rows), rows)
    out[...] = front[...] - jnp.dot(low_all[here, :], up_all[...], preferred_element_type=jnp.float32)


def product(front, lows, ups, starts):
    rows, width = front.shape
    children = ups[0].shape[0]
    depth = children * sum(up.shape[1] for up in ups)
    steps = 4
    block = pl.BlockSpec((rows // steps, width), lambda i, s: (i, 0))
    return pl.pallas_call(
        functools.partial(product_kernel, children, steps, len(lows), len(ups)),
        out_shape=jax.ShapeDtypeStruct((rows, width), jnp.float32),
        grid_spec=pltpu.PrefetchScalarGridSpec(
            num_scalar_prefetch=1,
            grid=(steps,),
            in_specs=[block] + [ANY] * (len(lows) + len(ups)),
            out_specs=block,
            scratch_shapes=[
                pltpu.VMEM((rows, depth), jnp.bfloat16),
                pltpu.VMEM((depth, width), jnp.bfloat16),
                pltpu.SemaphoreType.DMA((children * (len(lows) + len(ups)),)),
            ],
        ),
        compiler_params=pltpu.CompilerParams(vmem_limit_bytes=VMEM_LIMIT),
        cost_estimate=takes(15),
        name="product",
    )(starts, front, *lows, *ups)


class Relay:
    def __init__(self, block, count):
        self.inner = inner_factor(count)
        self.outer = count // self.inner
        self.z = lax.axis_index("row") // self.inner
        self.x = lax.axis_index("row") % self.inner
        self.up = self.down = block
        self.came = {}
        self.order = [
            [(k, d) for k in range(1, self.outer) for d in (1, -1) if 0 <= z - d * k < self.outer]
            for z in range(self.outer)
        ]
        self.held = [[block] + self.exchange(block, range(self.outer))]
        self.k = 0

    def send(self, x, moves, turn=0):
        n = self.inner
        return lax.ppermute(
            x, "row", [(z * n + i, to * n + (i + turn) % n) for z, to in moves.items() for i in range(n)]
        )

    def exchange(self, x, where):
        return [self.send(x, {z: z for z in where}, j) for j in range(1, self.inner)]

    def choose(self, number, where):
        names = {z: self.order[z][number - 1] for z in where}
        every = sorted(set(names.values()))
        block = self.came[every[0]]
        for name in every[1:]:
            here = functools.reduce(jnp.logical_or, [self.z == z for z in where if names[z] == name])
            block = jnp.where(here, self.came[name], block)
        return block

    def step(self):
        if self.k:
            block = self.choose(self.k, range(self.outer))
            self.held.append([block] + self.exchange(block, range(self.outer)))
        self.k += 1
        last = self.outer - 1
        if self.k == last:
            self.inside = self.choose(last, range(1, last))
            self.at_ends = self.send(self.inside, {1: 0, last - 1: last})
            return
        self.up = self.send(self.up, {z: z + 1 for z in range(self.k - 1, last)})
        self.down = self.send(self.down, {z: z - 1 for z in range(1, last - self.k + 2)})
        self.came[self.k, 1], self.came[self.k, -1] = self.up, self.down

    def pass_gate(self, arrays):
        mine = self.held[self.k - 1][1:]
        count = len(mine)
        self.up, self.down, *rest = gate([self.up, self.down, *mine, *arrays])
        self.came[self.k, 1], self.came[self.k, -1] = self.up, self.down
        self.held[self.k - 1][1:] = rest[:count]
        return rest[count:]

    def finish(self, arrays):
        mine = self.held[-1][1:]
        self.at_ends, *rest = gate([self.at_ends, *mine, *arrays])
        self.held[-1][1:] = rest[: len(mine)]
        block = jnp.where((self.z == 0) | (self.z == self.outer - 1), self.at_ends, self.inside)
        self.held.append([block] + self.exchange(block, range(self.outer)))
        return rest[len(mine) :]

    def blocks(self):
        found = []
        for k in range(self.outer):
            at = self.z
            if k:
                at = sum(
                    jnp.where(self.z == z, z - d * far, 0) for z, (far, d) in enumerate(o[k - 1] for o in self.order)
                )
            for j in range(self.inner):
                found.append((at * self.inner + (self.x - j + self.inner) % self.inner, self.held[k][j]))
        return found


def exchange_columns(found, bit):
    pairs = [(i, i ^ bit) for i in range(lax.axis_size("col"))]
    return found + [(far ^ bit, lax.ppermute(x, "col", pairs)) for far, x in found]


def shards(schur, lower, upper, tile_mask, row_map, front):
    children, rows, local_depth = lower.shape
    count = lax.axis_size("row")
    cap = 3 * rows // (2 * count)
    room = cap + NOTES
    row_tiles = rows // TILE
    pairs = local_depth // (2 * TILE)

    relay = Relay(upper, count)
    relay.step()

    target = row_map // rows
    place = row_map % rows
    earlier = jnp.tril(jnp.ones((rows, rows), jnp.bool_), -1)
    rank = jnp.sum((target[:, :, None] == target[:, None, :]) & earlier[None], axis=2, dtype=jnp.int32)
    picks = tile_mask.reshape(children, row_tiles, pairs, 2)[..., 1]
    code = jnp.sum(picks * (2 ** jnp.arange(pairs, dtype=jnp.int32)), axis=-1)
    code = jnp.repeat(code, TILE, axis=1)
    row_ids = jnp.broadcast_to(jnp.arange(rows, dtype=jnp.int32), (children, rows))
    digits = [place // BASE + 1, place % BASE, code, row_ids // BASE, row_ids % BASE]
    digits = [d.astype(jnp.bfloat16) for d in digits] + [row_unit(schur)[..., 0]]
    digits = jnp.stack(digits + [jnp.zeros_like(digits[0])] * (NOTES - len(digits)), axis=1)

    (digits,) = relay.pass_gate([digits])
    relay.step()
    sent_lower = lower_pack(lower, picks, target * room + rank, digits, count, room)
    notes = sent_lower[:, :, cap + 3 : cap + 5, :cap].astype(jnp.int32)
    source = (notes[:, :, 0] * BASE + notes[:, :, 1]).transpose(1, 0, 2).reshape(children, -1)
    sent = pack(schur, 0, source[0], count, None)
    while relay.k < relay.outer - 2:
        (sent,) = relay.pass_gate([sent])
        relay.step()
    sent_lower, sent, source = relay.pass_gate([sent_lower, sent, source])
    got_lower = lax.all_to_all(sent_lower, "row", split_axis=0, concat_axis=0, tiled=True)
    relay.step()
    for child in range(1, children):
        sent = pack(schur, child, source[child], count, sent)
    sent, got_lower = gate([sent, got_lower])
    got = lax.all_to_all(sent, "row", split_axis=0, concat_axis=0, tiled=True)

    notes = got_lower[:, :, cap : cap + NOTES, :cap].transpose(2, 1, 0, 3)
    got_place = notes[0].astype(jnp.int32) * BASE + notes[1].astype(jnp.int32) - BASE
    got_place = jnp.where(got_place >= 0, got_place, rows)
    spare = ((0, 0), (0, 0), (0, NOTES))
    full, units = lower_unpack(
        got_lower,
        rows,
        jnp.pad(got_place, spare, constant_values=rows),
        jnp.pad(notes[2].astype(jnp.float32), spare),
        jnp.pad(notes[5].astype(jnp.float32), spare),
    )

    full, units = relay.finish([full, units])
    column = lax.axis_index("col")
    bit = lax.axis_size("col")
    lows = [(0, full)]
    while bit > 1:
        bit //= 2
        lows = exchange_columns(lows, bit)
    ups = relay.blocks()
    starts = [(column ^ far) * local_depth for far, _ in lows] + [owner * upper.shape[1] for owner, _ in ups]
    result = product(front, [low for _, low in lows], [up for _, up in ups], jnp.stack(starts).astype(jnp.int32))
    return unpack(got, got_place, units, result)


def solution(mesh):
    in_specs = (
        P(None, "row", "col"),
        P(None, "row", "col"),
        P(None, "row", "col"),
        P(None, "row", "col"),
        P(None, "row"),
        P("row", "col"),
    )
    out_specs = P("row", "col")
    return jax.shard_map(shards, mesh=mesh, in_specs=in_specs, out_specs=out_specs, check_vma=False)
```

```python
import functools

import jax
import jax.numpy as jnp
from jax import lax
from jax.experimental import pallas as pl
from jax.experimental.pallas import tpu as pltpu
from jax.sharding import PartitionSpec as P

TILE = 128
LANES = 128
TOP = 32767.0
STEP = (1.0 + 2.0**-7) / TOP
NOTES = 16
BASE = 32
TINY = 1e-33
VMEM_LIMIT = 56 * 1024 * 1024
ANY = pl.BlockSpec(memory_space=pl.ANY)


def inner_factor(count):
    inner = 1
    while (2 * inner) * (2 * inner) <= count:
        inner *= 2
    return inner


def takes(us):
    return pl.CostEstimate(flops=int(us * 4e9), bytes_accessed=int(us * 3.3e6), transcendentals=0)


def gate_kernel(*refs):
    pass


def gate(arrays, *first):
    count = len(arrays)
    return pl.pallas_call(
        gate_kernel,
        out_shape=[jax.ShapeDtypeStruct(x.shape, x.dtype) for x in arrays],
        in_specs=[ANY] * (count + len(first)),
        out_specs=[ANY] * count,
        input_output_aliases={i: i for i in range(count)},
        name="gate",
    )(*arrays, *first)


def row_unit(x):
    most = jnp.max(jnp.abs(x), axis=-1, keepdims=True)
    return jnp.where(most > TINY, most * STEP, 0.0).astype(jnp.bfloat16)


def pack_kernel(groups, steps, source, x, *refs):
    out, held = refs[-2:]
    i = pl.program_id(0)
    rows = x.shape[1]
    targets, _, tiles = out.shape[:3]
    per = 16 // groups

    @pl.when(i < steps)
    def _():
        def body(g, carry):
            at = pl.multiple_of(g * 8, 8)
            v = x[0, pl.ds(at, 8), :]
            unit = row_unit(v).astype(jnp.float32)
            inverse = jnp.where(unit > 0.0, 1.0 / unit, 0.0)
            q = jnp.floor(v * inverse + 0.5).astype(jnp.int32)
            base = (i * rows + at) * groups
            for j in range(groups):
                held[pl.ds(base + j, 8, stride=groups), :] = q[:, j * LANES : (j + 1) * LANES]
            return carry

        lax.fori_loop(0, rows // 8, body, 0, unroll=4)

    @pl.when(i >= steps)
    def _():
        for target in range(targets):
            start = ((i - steps) * targets + target) * tiles * per

            def body(t, carry):
                parts = []
                for a in range(per):
                    row = pl.multiple_of(source[start + t * per + a] * groups, groups)
                    parts.append(held[pl.ds(row, groups), :])
                out[target, 0, t] = jnp.concatenate(parts, axis=0).astype(jnp.int16)
                return carry

            lax.fori_loop(0, tiles, body, 0, unroll=8)


def pack(x, child, source, count, into, *first):
    children, rows, width = x.shape
    cap = source.shape[0] // count
    groups = width // LANES
    tiles = cap * groups // 16
    steps, out_steps = 2, 4
    first = first if into is None else (into,) + first
    return pl.pallas_call(
        functools.partial(pack_kernel, groups, steps),
        out_shape=jax.ShapeDtypeStruct((count, children, tiles, 16, LANES), jnp.int16),
        grid_spec=pltpu.PrefetchScalarGridSpec(
            num_scalar_prefetch=1,
            grid=(steps + out_steps,),
            in_specs=[pl.BlockSpec((1, rows // steps, width), lambda i, s: (child, jnp.minimum(i, steps - 1), 0))]
            + [ANY] * len(first),
            out_specs=pl.BlockSpec(
                (count // out_steps, 1, tiles, 16, LANES),
                lambda i, s: (jnp.maximum(i - steps, 0), child, 0, 0, 0),
            ),
            scratch_shapes=[pltpu.VMEM((rows * groups, LANES), jnp.int32)],
        ),
        input_output_aliases={} if into is None else {2: 0},
        compiler_params=pltpu.CompilerParams(vmem_limit_bytes=VMEM_LIMIT),
        cost_estimate=takes(10),
        name="pack",
    )(source, x, *first)


def unpack_kernel(groups, parts, row_at, valid, got, before, unit, out, held):
    i = pl.program_id(0)
    children = unit.shape[0]
    per = 16 // groups
    chunk = 16
    tiles = got.shape[2]

    @pl.when(i < parts)
    def _():
        for c, s in [(c, s) for s in range(got.shape[0]) for c in range(children)]:
            device = i * got.shape[0] + s
            number = c * parts * got.shape[0] + device
            base = number * tiles * per

            def body(k, carry):
                for t in range(chunk // per):
                    v = got[s, c, k * (chunk // per) + t].astype(jnp.int32).astype(jnp.float32)
                    for a in range(per):
                        row = pl.multiple_of(row_at[base + k * chunk + t * per + a], groups)
                        held[c, pl.ds(row, groups), :] = v[a * groups : (a + 1) * groups]
                return carry

            lax.fori_loop(0, (valid[number] + chunk - 1) // chunk, body, 0)

    @pl.when(i >= parts)
    def _():
        rows = out.shape[0]

        def body(g, carry):
            at = pl.multiple_of(g * 8, 8)
            base = ((i - parts) * rows + at) * groups
            for j in range(groups):
                cols = pl.ds(j * LANES, LANES)
                total = before[pl.ds(at, 8), cols]
                for c in range(children):
                    total += held[c, pl.ds(base + j, 8, stride=groups), :] * unit[c, pl.ds(at, 8), :]
                out[pl.ds(at, 8), cols] = total
            return carry

        lax.fori_loop(0, rows // 8, body, 0, unroll=2)


def unpack(got, place, unit, before):
    rows, width = before.shape
    count, children, tiles = got.shape[:3]
    groups = width // LANES
    steps, out_steps = count // 2, 2

    def block(i, *_):
        return jnp.maximum(i - steps, 0), 0

    valid = jnp.sum(place < rows, axis=2, dtype=jnp.int32)
    return pl.pallas_call(
        functools.partial(unpack_kernel, groups, steps),
        out_shape=jax.ShapeDtypeStruct((rows, width), jnp.float32),
        grid_spec=pltpu.PrefetchScalarGridSpec(
            num_scalar_prefetch=2,
            grid=(steps + out_steps,),
            in_specs=[
                pl.BlockSpec(
                    (count // steps, children, tiles, 16, LANES), lambda i, *_: (jnp.minimum(i, steps - 1), 0, 0, 0, 0)
                ),
                pl.BlockSpec((rows // out_steps, width), block),
                pl.BlockSpec((children, rows // out_steps, LANES), lambda i, *_: (0, block(i)[0], 0)),
            ],
            out_specs=pl.BlockSpec((rows // out_steps, width), block),
            scratch_shapes=[pltpu.VMEM((children, (rows + 8) * groups, LANES), jnp.float32)],
        ),
        compiler_params=pltpu.CompilerParams(vmem_limit_bytes=VMEM_LIMIT),
        cost_estimate=takes(11),
        name="unpack",
    )((place * groups).reshape(-1), valid.reshape(-1), got, before, unit)


def lower_pack_kernel(picks, low, slot, digits, out, compact):
    c = pl.program_id(0)
    rows, wide = compact.shape
    pairs = wide // TILE
    count, _, room, _ = out.shape
    for i in range(rows // TILE):
        for j in range(pairs):
            column = (2 * j + picks[(c * (rows // TILE) + i) * pairs + j]) * TILE
            at = pl.ds(i * TILE, TILE)
            compact[at, j * TILE : (j + 1) * TILE] = low[0, at, pl.ds(pl.multiple_of(column, TILE), TILE)]

    def body(t, carry):
        ids = lax.broadcasted_iota(jnp.int32, (max(room, wide), rows), 0) + t * room
        hit = jnp.where(slot[0] == ids, 1.0, 0.0).astype(jnp.bfloat16)
        mine = jnp.dot(hit[:room], compact[...], preferred_element_type=jnp.float32)
        out[t, 0] = mine.astype(jnp.bfloat16)
        notes = lax.dot_general(
            digits[0], hit[:wide], (((1,), (1,)), ((), ())), preferred_element_type=jnp.float32
        )
        out[t, 0, room - NOTES :, :] = notes.astype(jnp.bfloat16)
        return carry

    lax.fori_loop(0, count, body, 0)


def lower_pack(lower, picks, slot, digits, count, room):
    children, rows, depth = lower.shape
    wide = depth // 2
    return pl.pallas_call(
        lower_pack_kernel,
        out_shape=jax.ShapeDtypeStruct((count, children, room, wide), jnp.bfloat16),
        grid_spec=pltpu.PrefetchScalarGridSpec(
            num_scalar_prefetch=1,
            grid=(children,),
            in_specs=[
                pl.BlockSpec((1, rows, depth), lambda c, p: (c, 0, 0)),
                pl.BlockSpec((1, 1, rows), lambda c, p: (c, 0, 0)),
                pl.BlockSpec((1, NOTES, rows), lambda c, p: (c, 0, 0)),
            ],
            out_specs=pl.BlockSpec((count, 1, room, wide), lambda c, p: (0, c, 0, 0)),
            scratch_shapes=[pltpu.VMEM((rows, wide), jnp.bfloat16)],
        ),
        compiler_params=pltpu.CompilerParams(vmem_limit_bytes=VMEM_LIMIT),
        cost_estimate=takes(7),
        name="lower_pack",
    )(picks.reshape(-1), lower, slot.reshape(children, 1, rows), digits)


def lower_unpack_kernel(got, place, code, unit, out, units):
    count, _, room, wide = got.shape
    slots = count * room
    rows = out.shape[1]
    step = 256

    def body(t, carry):
        at = pl.multiple_of(t * step, step)
        ids = lax.broadcasted_iota(jnp.int32, (step, slots), 0) + at
        hit = place[0] == ids
        mine = jnp.dot(
            jnp.where(hit, 1.0, 0.0).astype(jnp.bfloat16),
            got[...].reshape(slots, wide),
            preferred_element_type=jnp.float32,
        )
        bits = jnp.sum(jnp.where(hit, code[0], 0.0), axis=1, keepdims=True).astype(jnp.int32)
        row = jnp.sum(jnp.where(hit, unit[0], 0.0), axis=1, keepdims=True)
        units[0, pl.ds(at, step), :] = jnp.broadcast_to(row, (step, LANES))
        for j in range(wide // TILE):
            bit = (bits >> j) & 1
            for s in range(2):
                tile = jnp.where(bit == s, mine[:, j * TILE : (j + 1) * TILE], 0.0)
                out[0, pl.ds(at, step), (2 * j + s) * TILE : (2 * j + s + 1) * TILE] = tile.astype(jnp.bfloat16)
        return carry

    lax.fori_loop(0, rows // step, body, 0)


def lower_unpack(got, rows, *lanes):
    count, children, room, wide = got.shape
    slots = count * room
    lane = pl.BlockSpec((1, 1, slots), lambda c: (c, 0, 0))
    whole = lambda n: pl.BlockSpec((1, rows, n), lambda c: (c, 0, 0))
    return pl.pallas_call(
        lower_unpack_kernel,
        out_shape=(
            jax.ShapeDtypeStruct((children, rows, 2 * wide), jnp.bfloat16),
            jax.ShapeDtypeStruct((children, rows, LANES), jnp.float32),
        ),
        grid=(children,),
        in_specs=[pl.BlockSpec((count, 1, room, wide), lambda c: (0, c, 0, 0))] + [lane] * len(lanes),
        out_specs=(whole(2 * wide), whole(LANES)),
        compiler_params=pltpu.CompilerParams(vmem_limit_bytes=VMEM_LIMIT),
        cost_estimate=takes(5),
        name="lower_unpack",
    )(got, *[x.reshape(children, 1, slots) for x in lanes])


def product_kernel(children, steps, parts, blocks, starts, front, *refs):
    lows, ups = refs[:parts], refs[parts : parts + blocks]
    out, low_all, up_all, sems = refs[parts + blocks :]
    i = pl.program_id(0)
    rows = front.shape[0]
    depth = low_all.shape[1] // children

    @pl.when(i == 0)
    def _():
        copies = []
        for c in range(children):
            for n, low in enumerate(lows):
                at = pl.ds(pl.multiple_of(c * depth + starts[n], low.shape[2]), low.shape[2])
                copies.append(pltpu.make_async_copy(low.at[c], low_all.at[:, at], sems.at[len(copies)]))
            for n, up in enumerate(ups):
                at = pl.ds(pl.multiple_of(c * depth + starts[parts + n], up.shape[1]), up.shape[1])
                copies.append(pltpu.make_async_copy(up.at[c], up_all.at[at], sems.at[len(copies)]))
        for copy in copies:
            copy.start()
        for copy in copies:
            copy.wait()

    here = pl.ds(pl.multiple_of(i * rows, rows), rows)
    out[...] = front[...] - jnp.dot(low_all[here, :], up_all[...], preferred_element_type=jnp.float32)


def product(front, lows, ups, starts):
    rows, width = front.shape
    children = ups[0].shape[0]
    depth = children * sum(up.shape[1] for up in ups)
    steps = 4
    block = pl.BlockSpec((rows // steps, width), lambda i, s: (i, 0))
    return pl.pallas_call(
        functools.partial(product_kernel, children, steps, len(lows), len(ups)),
        out_shape=jax.ShapeDtypeStruct((rows, width), jnp.float32),
        grid_spec=pltpu.PrefetchScalarGridSpec(
            num_scalar_prefetch=1,
            grid=(steps,),
            in_specs=[block] + [ANY] * (len(lows) + len(ups)),
            out_specs=block,
            scratch_shapes=[
                pltpu.VMEM((rows, depth), jnp.bfloat16),
                pltpu.VMEM((depth, width), jnp.bfloat16),
                pltpu.SemaphoreType.DMA((children * (len(lows) + len(ups)),)),
            ],
        ),
        compiler_params=pltpu.CompilerParams(vmem_limit_bytes=VMEM_LIMIT),
        cost_estimate=takes(15),
        name="product",
    )(starts, front, *lows, *ups)


class Relay:
    def __init__(self, block, count):
        self.inner = inner_factor(count)
        self.outer = count // self.inner
        self.z = lax.axis_index("row") // self.inner
        self.x = lax.axis_index("row") % self.inner
        self.up = self.down = block
        self.came = {}
        self.order = [
            [(k, d) for k in range(1, self.outer) for d in (1, -1) if 0 <= z - d * k < self.outer]
            for z in range(self.outer)
        ]
        self.held = [[block] + self.exchange(block, range(self.outer))]
        self.k = 0

    def send(self, x, moves, turn=0):
        n = self.inner
        return lax.ppermute(
            x, "row", [(z * n + i, to * n + (i + turn) % n) for z, to in moves.items() for i in range(n)]
        )

    def exchange(self, x, where):
        return [self.send(x, {z: z for z in where}, j) for j in range(1, self.inner)]

    def choose(self, number, where):
        names = {z: self.order[z][number - 1] for z in where}
        every = sorted(set(names.values()))
        block = self.came[every[0]]
        for name in every[1:]:
            here = functools.reduce(jnp.logical_or, [self.z == z for z in where if names[z] == name])
            block = jnp.where(here, self.came[name], block)
        return block

    def step(self):
        if self.k:
            block = self.choose(self.k, range(self.outer))
            self.held.append([block] + self.exchange(block, range(self.outer)))
        self.k += 1
        last = self.outer - 1
        if self.k == last:
            self.inside = self.choose(last, range(1, last))
            self.at_ends = self.send(self.inside, {1: 0, last - 1: last})
            return
        self.up = self.send(self.up, {z: z + 1 for z in range(self.k - 1, last)})
        self.down = self.send(self.down, {z: z - 1 for z in range(1, last - self.k + 2)})
        self.came[self.k, 1], self.came[self.k, -1] = self.up, self.down

    def pass_gate(self, arrays):
        mine = self.held[self.k - 1][1:]
        count = len(mine)
        self.up, self.down, *rest = gate([self.up, self.down, *mine, *arrays])
        self.came[self.k, 1], self.came[self.k, -1] = self.up, self.down
        self.held[self.k - 1][1:] = rest[:count]
        return rest[count:]

    def finish(self, arrays):
        mine = self.held[-1][1:]
        self.at_ends, *rest = gate([self.at_ends, *mine, *arrays])
        self.held[-1][1:] = rest[: len(mine)]
        block = jnp.where((self.z == 0) | (self.z == self.outer - 1), self.at_ends, self.inside)
        self.held.append([block] + self.exchange(block, range(self.outer)))
        return rest[len(mine) :]

    def blocks(self):
        found = []
        for k in range(self.outer):
            at = self.z
            if k:
                at = sum(
                    jnp.where(self.z == z, z - d * far, 0) for z, (far, d) in enumerate(o[k - 1] for o in self.order)
                )
            for j in range(self.inner):
                found.append((at * self.inner + (self.x - j + self.inner) % self.inner, self.held[k][j]))
        return found


def exchange_columns(found, bit):
    pairs = [(i, i ^ bit) for i in range(lax.axis_size("col"))]
    return found + [(far ^ bit, lax.ppermute(x, "col", pairs)) for far, x in found]


def shards(schur, lower, upper, tile_mask, row_map, front):
    children, rows, local_depth = lower.shape
    count = lax.axis_size("row")
    cap = 3 * rows // (2 * count)
    room = cap + NOTES
    row_tiles = rows // TILE
    pairs = local_depth // (2 * TILE)

    relay = Relay(upper, count)
    relay.step()

    target = row_map // rows
    place = row_map % rows
    earlier = jnp.tril(jnp.ones((rows, rows), jnp.bool_), -1)
    rank = jnp.sum((target[:, :, None] == target[:, None, :]) & earlier[None], axis=2, dtype=jnp.int32)
    picks = tile_mask.reshape(children, row_tiles, pairs, 2)[..., 1]
    code = jnp.sum(picks * (2 ** jnp.arange(pairs, dtype=jnp.int32)), axis=-1)
    code = jnp.repeat(code, TILE, axis=1)
    row_ids = jnp.broadcast_to(jnp.arange(rows, dtype=jnp.int32), (children, rows))
    digits = [place // BASE + 1, place % BASE, code, row_ids // BASE, row_ids % BASE]
    digits = [d.astype(jnp.bfloat16) for d in digits] + [row_unit(schur)[..., 0]]
    digits = jnp.stack(digits + [jnp.zeros_like(digits[0])] * (NOTES - len(digits)), axis=1)

    sent_lower = lower_pack(lower, picks, target * room + rank, digits, count, room)
    notes = sent_lower[:, :, cap + 3 : cap + 5, :cap].astype(jnp.int32)
    source = (notes[:, :, 0] * BASE + notes[:, :, 1]).transpose(1, 0, 2).reshape(children, -1)

    sent_lower, source = relay.pass_gate([sent_lower, source])
    relay.step()
    sent = pack(schur, 0, source[0], count, None)
    sent_lower, sent = gate([sent_lower, sent])
    got_lower = lax.all_to_all(sent_lower, "row", split_axis=0, concat_axis=0, tiled=True)
    while relay.k < relay.outer - 2:
        (sent,) = relay.pass_gate([sent])
        relay.step()
    (sent,) = relay.pass_gate([sent])
    relay.step()
    for child in range(1, children):
        sent = pack(schur, child, source[child], count, sent)
    sent, got_lower = gate([sent, got_lower])
    got = lax.all_to_all(sent, "row", split_axis=0, concat_axis=0, tiled=True)

    notes = got_lower[:, :, cap : cap + NOTES, :cap].transpose(2, 1, 0, 3)
    got_place = notes[0].astype(jnp.int32) * BASE + notes[1].astype(jnp.int32) - BASE
    got_place = jnp.where(got_place >= 0, got_place, rows)
    spare = ((0, 0), (0, 0), (0, NOTES))
    full, units = lower_unpack(
        got_lower,
        rows,
        jnp.pad(got_place, spare, constant_values=rows),
        jnp.pad(notes[2].astype(jnp.float32), spare),
        jnp.pad(notes[5].astype(jnp.float32), spare),
    )

    full, units = relay.finish([full, units])
    column = lax.axis_index("col")
    bit = lax.axis_size("col")
    lows = [(0, full)]
    while bit > 1:
        bit //= 2
        lows = exchange_columns(lows, bit)
    ups = relay.blocks()
    starts = [(column ^ far) * local_depth for far, _ in lows] + [owner * upper.shape[1] for owner, _ in ups]
    result = product(front, [low for _, low in lows], [up for _, up in ups], jnp.stack(starts).astype(jnp.int32))
    return unpack(got, got_place, units, result)


def solution(mesh):
    in_specs = (
        P(None, "row", "col"),
        P(None, "row", "col"),
        P(None, "row", "col"),
        P(None, "row", "col"),
        P(None, "row"),
        P("row", "col"),
    )
    out_specs = P("row", "col")
    return jax.shard_map(shards, mesh=mesh, in_specs=in_specs, out_specs=out_specs, check_vma=False)
```

```python
import functools

import jax
import jax.numpy as jnp
from jax import lax
from jax.experimental import pallas as pl
from jax.experimental.pallas import tpu as pltpu
from jax.sharding import PartitionSpec as P

TILE = 128
LANES = 128
TOP = 32767.0
STEP = (1.0 + 2.0**-7) / TOP
NOTES = 16
BASE = 32
TINY = 1e-33
VMEM_LIMIT = 56 * 1024 * 1024
ANY = pl.BlockSpec(memory_space=pl.ANY)


def inner_factor(count):
    inner = 1
    while (2 * inner) * (2 * inner) <= count:
        inner *= 2
    return inner


def takes(us):
    return pl.CostEstimate(flops=int(us * 4e9), bytes_accessed=int(us * 3.3e6), transcendentals=0)


def gate_kernel(*refs):
    pass


def gate(arrays, *first):
    count = len(arrays)
    return pl.pallas_call(
        gate_kernel,
        out_shape=[jax.ShapeDtypeStruct(x.shape, x.dtype) for x in arrays],
        in_specs=[ANY] * (count + len(first)),
        out_specs=[ANY] * count,
        input_output_aliases={i: i for i in range(count)},
        name="gate",
    )(*arrays, *first)


def row_unit(x):
    most = jnp.max(jnp.abs(x), axis=-1, keepdims=True)
    return jnp.where(most > TINY, most * STEP, 0.0).astype(jnp.bfloat16)


def pack_kernel(groups, steps, source, x, *refs):
    out, held, scale = refs[-3:]
    i = pl.program_id(0)
    rows = x.shape[1]
    targets, _, tiles = out.shape[:3]
    per = 16 // groups

    @pl.when(i < steps)
    def _():
        unit = row_unit(x[0]).astype(jnp.float32)
        scale[...] = jnp.broadcast_to(jnp.where(unit > 0.0, 1.0 / unit, 0.0), scale.shape)

        def body(g, carry):
            at = pl.multiple_of(g * 8, 8)
            inverse = scale[pl.ds(at, 8), :]
            base = (i * rows + at) * groups
            for j in range(groups):
                v = x[0, pl.ds(at, 8), j * LANES : (j + 1) * LANES]
                held[pl.ds(base + j, 8, stride=groups), :] = jnp.floor(v * inverse + 0.5).astype(jnp.int32)
            return carry

        lax.fori_loop(0, rows // 8, body, 0, unroll=4)

    @pl.when(i >= steps)
    def _():
        for target in range(targets):
            start = ((i - steps) * targets + target) * tiles * per

            def body(t, carry):
                parts = []
                for a in range(per):
                    row = pl.multiple_of(source[start + t * per + a] * groups, groups)
                    parts.append(held[pl.ds(row, groups), :])
                out[target, 0, t] = jnp.concatenate(parts, axis=0).astype(jnp.int16)
                return carry

            lax.fori_loop(0, tiles, body, 0, unroll=8)


def pack(x, child, source, count, into, *first):
    children, rows, width = x.shape
    cap = source.shape[0] // count
    groups = width // LANES
    tiles = cap * groups // 16
    steps, out_steps = 2, 4
    first = first if into is None else (into,) + first
    return pl.pallas_call(
        functools.partial(pack_kernel, groups, steps),
        out_shape=jax.ShapeDtypeStruct((count, children, tiles, 16, LANES), jnp.int16),
        grid_spec=pltpu.PrefetchScalarGridSpec(
            num_scalar_prefetch=1,
            grid=(steps + out_steps,),
            in_specs=[pl.BlockSpec((1, rows // steps, width), lambda i, s: (child, jnp.minimum(i, steps - 1), 0))]
            + [ANY] * len(first),
            out_specs=pl.BlockSpec(
                (count // out_steps, 1, tiles, 16, LANES),
                lambda i, s: (jnp.maximum(i - steps, 0), child, 0, 0, 0),
            ),
            scratch_shapes=[
                pltpu.VMEM((rows * groups, LANES), jnp.int32),
                pltpu.VMEM((rows // steps, LANES), jnp.float32),
            ],
        ),
        input_output_aliases={} if into is None else {2: 0},
        compiler_params=pltpu.CompilerParams(vmem_limit_bytes=VMEM_LIMIT),
        cost_estimate=takes(10),
        name="pack",
    )(source, x, *first)


def unpack_kernel(groups, parts, row_at, valid, got, before, unit, out, held):
    i = pl.program_id(0)
    children = unit.shape[0]
    per = 16 // groups
    chunk = 16
    tiles = got.shape[2]

    @pl.when(i < parts)
    def _():
        for c, s in [(c, s) for s in range(got.shape[0]) for c in range(children)]:
            device = i * got.shape[0] + s
            number = c * parts * got.shape[0] + device
            base = number * tiles * per

            def body(k, carry):
                for t in range(chunk // per):
                    v = got[s, c, k * (chunk // per) + t].astype(jnp.int32).astype(jnp.float32)
                    for a in range(per):
                        row = pl.multiple_of(row_at[base + k * chunk + t * per + a], groups)
                        held[c, pl.ds(row, groups), :] = v[a * groups : (a + 1) * groups]
                return carry

            lax.fori_loop(0, (valid[number] + chunk - 1) // chunk, body, 0)

    @pl.when(i >= parts)
    def _():
        rows = out.shape[0]

        def body(g, carry):
            at = pl.multiple_of(g * 8, 8)
            base = ((i - parts) * rows + at) * groups
            for j in range(groups):
                cols = pl.ds(j * LANES, LANES)
                total = before[pl.ds(at, 8), cols]
                for c in range(children):
                    total += held[c, pl.ds(base + j, 8, stride=groups), :] * unit[c, pl.ds(at, 8), :]
                out[pl.ds(at, 8), cols] = total
            return carry

        lax.fori_loop(0, rows // 8, body, 0, unroll=2)


def unpack(got, place, unit, before):
    rows, width = before.shape
    count, children, tiles = got.shape[:3]
    groups = width // LANES
    steps, out_steps = count // 4, 2

    def block(i, *_):
        return jnp.maximum(i - steps, 0), 0

    valid = jnp.sum(place < rows, axis=2, dtype=jnp.int32)
    return pl.pallas_call(
        functools.partial(unpack_kernel, groups, steps),
        out_shape=jax.ShapeDtypeStruct((rows, width), jnp.float32),
        grid_spec=pltpu.PrefetchScalarGridSpec(
            num_scalar_prefetch=2,
            grid=(steps + out_steps,),
            in_specs=[
                pl.BlockSpec(
                    (count // steps, children, tiles, 16, LANES), lambda i, *_: (jnp.minimum(i, steps - 1), 0, 0, 0, 0)
                ),
                pl.BlockSpec((rows // out_steps, width), block),
                pl.BlockSpec((children, rows // out_steps, LANES), lambda i, *_: (0, block(i)[0], 0)),
            ],
            out_specs=pl.BlockSpec((rows // out_steps, width), block),
            scratch_shapes=[pltpu.VMEM((children, (rows + 8) * groups, LANES), jnp.float32)],
        ),
        compiler_params=pltpu.CompilerParams(vmem_limit_bytes=VMEM_LIMIT),
        cost_estimate=takes(11),
        name="unpack",
    )((place * groups).reshape(-1), valid.reshape(-1), got, before, unit)


def lower_pack_kernel(picks, low, slot, digits, out, compact):
    c = pl.program_id(0)
    rows, wide = compact.shape
    pairs = wide // TILE
    count, _, room, _ = out.shape
    for i in range(rows // TILE):
        for j in range(pairs):
            column = (2 * j + picks[(c * (rows // TILE) + i) * pairs + j]) * TILE
            at = pl.ds(i * TILE, TILE)
            compact[at, j * TILE : (j + 1) * TILE] = low[0, at, pl.ds(pl.multiple_of(column, TILE), TILE)]

    def body(t, carry):
        ids = lax.broadcasted_iota(jnp.int32, (max(room, wide), rows), 0) + t * room
        hit = jnp.where(slot[0] == ids, 1.0, 0.0).astype(jnp.bfloat16)
        mine = jnp.dot(hit[:room], compact[...], preferred_element_type=jnp.float32)
        out[t, 0] = mine.astype(jnp.bfloat16)
        notes = lax.dot_general(
            digits[0], hit[:wide], (((1,), (1,)), ((), ())), preferred_element_type=jnp.float32
        )
        out[t, 0, room - NOTES :, :] = notes.astype(jnp.bfloat16)
        return carry

    lax.fori_loop(0, count, body, 0)


def lower_pack(lower, picks, slot, digits, count, room):
    children, rows, depth = lower.shape
    wide = depth // 2
    return pl.pallas_call(
        lower_pack_kernel,
        out_shape=jax.ShapeDtypeStruct((count, children, room, wide), jnp.bfloat16),
        grid_spec=pltpu.PrefetchScalarGridSpec(
            num_scalar_prefetch=1,
            grid=(children,),
            in_specs=[
                pl.BlockSpec((1, rows, depth), lambda c, p: (c, 0, 0)),
                pl.BlockSpec((1, 1, rows), lambda c, p: (c, 0, 0)),
                pl.BlockSpec((1, NOTES, rows), lambda c, p: (c, 0, 0)),
            ],
            out_specs=pl.BlockSpec((count, 1, room, wide), lambda c, p: (0, c, 0, 0)),
            scratch_shapes=[pltpu.VMEM((rows, wide), jnp.bfloat16)],
        ),
        compiler_params=pltpu.CompilerParams(vmem_limit_bytes=VMEM_LIMIT),
        cost_estimate=takes(7),
        name="lower_pack",
    )(picks.reshape(-1), lower, slot.reshape(children, 1, rows), digits)


def lower_unpack_kernel(got, place, code, unit, out, units):
    count, _, room, wide = got.shape
    slots = count * room
    rows = out.shape[1]
    step = 256

    def body(t, carry):
        at = pl.multiple_of(t * step, step)
        ids = lax.broadcasted_iota(jnp.int32, (step, slots), 0) + at
        hit = place[0] == ids
        mine = jnp.dot(
            jnp.where(hit, 1.0, 0.0).astype(jnp.bfloat16),
            got[...].reshape(slots, wide),
            preferred_element_type=jnp.float32,
        )
        bits = jnp.sum(jnp.where(hit, code[0], 0.0), axis=1, keepdims=True).astype(jnp.int32)
        row = jnp.sum(jnp.where(hit, unit[0], 0.0), axis=1, keepdims=True)
        units[0, pl.ds(at, step), :] = jnp.broadcast_to(row, (step, LANES))
        for j in range(wide // TILE):
            bit = (bits >> j) & 1
            for s in range(2):
                tile = jnp.where(bit == s, mine[:, j * TILE : (j + 1) * TILE], 0.0)
                out[0, pl.ds(at, step), (2 * j + s) * TILE : (2 * j + s + 1) * TILE] = tile.astype(jnp.bfloat16)
        return carry

    lax.fori_loop(0, rows // step, body, 0)


def lower_unpack(got, rows, *lanes):
    count, children, room, wide = got.shape
    slots = count * room
    lane = pl.BlockSpec((1, 1, slots), lambda c: (c, 0, 0))
    whole = lambda n: pl.BlockSpec((1, rows, n), lambda c: (c, 0, 0))
    return pl.pallas_call(
        lower_unpack_kernel,
        out_shape=(
            jax.ShapeDtypeStruct((children, rows, 2 * wide), jnp.bfloat16),
            jax.ShapeDtypeStruct((children, rows, LANES), jnp.float32),
        ),
        grid=(children,),
        in_specs=[pl.BlockSpec((count, 1, room, wide), lambda c: (0, c, 0, 0))] + [lane] * len(lanes),
        out_specs=(whole(2 * wide), whole(LANES)),
        compiler_params=pltpu.CompilerParams(vmem_limit_bytes=VMEM_LIMIT),
        cost_estimate=takes(5),
        name="lower_unpack",
    )(got, *[x.reshape(children, 1, slots) for x in lanes])


def product_kernel(children, steps, parts, blocks, starts, front, *refs):
    lows, ups = refs[:parts], refs[parts : parts + blocks]
    out, low_all, up_all, sems = refs[parts + blocks :]
    i = pl.program_id(0)
    rows = front.shape[0]
    depth = low_all.shape[1] // children

    @pl.when(i == 0)
    def _():
        copies = []
        for c in range(children):
            for n, low in enumerate(lows):
                at = pl.ds(pl.multiple_of(c * depth + starts[n], low.shape[2]), low.shape[2])
                copies.append(pltpu.make_async_copy(low.at[c], low_all.at[:, at], sems.at[len(copies)]))
            for n, up in enumerate(ups):
                at = pl.ds(pl.multiple_of(c * depth + starts[parts + n], up.shape[1]), up.shape[1])
                copies.append(pltpu.make_async_copy(up.at[c], up_all.at[at], sems.at[len(copies)]))
        for copy in copies:
            copy.start()
        for copy in copies:
            copy.wait()

    here = pl.ds(pl.multiple_of(i * rows, rows), rows)
    out[...] = front[...] - jnp.dot(low_all[here, :], up_all[...], preferred_element_type=jnp.float32)


def product(front, lows, ups, starts):
    rows, width = front.shape
    children = ups[0].shape[0]
    depth = children * sum(up.shape[1] for up in ups)
    steps = 4
    block = pl.BlockSpec((rows // steps, width), lambda i, s: (i, 0))
    return pl.pallas_call(
        functools.partial(product_kernel, children, steps, len(lows), len(ups)),
        out_shape=jax.ShapeDtypeStruct((rows, width), jnp.float32),
        grid_spec=pltpu.PrefetchScalarGridSpec(
            num_scalar_prefetch=1,
            grid=(steps,),
            in_specs=[block] + [ANY] * (len(lows) + len(ups)),
            out_specs=block,
            scratch_shapes=[
                pltpu.VMEM((rows, depth), jnp.bfloat16),
                pltpu.VMEM((depth, width), jnp.bfloat16),
                pltpu.SemaphoreType.DMA((children * (len(lows) + len(ups)),)),
            ],
        ),
        compiler_params=pltpu.CompilerParams(vmem_limit_bytes=VMEM_LIMIT),
        cost_estimate=takes(15),
        name="product",
    )(starts, front, *lows, *ups)


class Relay:
    def __init__(self, block, count):
        self.inner = inner_factor(count)
        self.outer = count // self.inner
        self.z = lax.axis_index("row") // self.inner
        self.x = lax.axis_index("row") % self.inner
        self.up = self.down = block
        self.came = {}
        self.order = [
            [(k, d) for k in range(1, self.outer) for d in (1, -1) if 0 <= z - d * k < self.outer]
            for z in range(self.outer)
        ]
        self.held = [[block] + self.exchange(block, range(self.outer))]
        self.k = 0

    def send(self, x, moves, turn=0):
        n = self.inner
        return lax.ppermute(
            x, "row", [(z * n + i, to * n + (i + turn) % n) for z, to in moves.items() for i in range(n)]
        )

    def exchange(self, x, where):
        return [self.send(x, {z: z for z in where}, j) for j in range(1, self.inner)]

    def choose(self, number, where):
        names = {z: self.order[z][number - 1] for z in where}
        every = sorted(set(names.values()))
        block = self.came[every[0]]
        for name in every[1:]:
            here = functools.reduce(jnp.logical_or, [self.z == z for z in where if names[z] == name])
            block = jnp.where(here, self.came[name], block)
        return block

    def step(self):
        if self.k:
            block = self.choose(self.k, range(self.outer))
            self.held.append([block] + self.exchange(block, range(self.outer)))
        self.k += 1
        last = self.outer - 1
        if self.k == last:
            self.inside = self.choose(last, range(1, last))
            self.at_ends = self.send(self.inside, {1: 0, last - 1: last})
            return
        self.up = self.send(self.up, {z: z + 1 for z in range(self.k - 1, last)})
        self.down = self.send(self.down, {z: z - 1 for z in range(1, last - self.k + 2)})
        self.came[self.k, 1], self.came[self.k, -1] = self.up, self.down

    def pass_gate(self, arrays):
        mine = self.held[self.k - 1][1:]
        count = len(mine)
        self.up, self.down, *rest = gate([self.up, self.down, *mine, *arrays])
        self.came[self.k, 1], self.came[self.k, -1] = self.up, self.down
        self.held[self.k - 1][1:] = rest[:count]
        return rest[count:]

    def finish(self, arrays):
        mine = self.held[-1][1:]
        self.at_ends, *rest = gate([self.at_ends, *mine, *arrays])
        self.held[-1][1:] = rest[: len(mine)]
        block = jnp.where((self.z == 0) | (self.z == self.outer - 1), self.at_ends, self.inside)
        self.held.append([block] + self.exchange(block, range(self.outer)))
        return rest[len(mine) :]

    def finish_along_x(self, arrays):
        mine = self.held[-1][1:]
        rest = gate([*mine, *arrays])
        self.held[-1][1:] = rest[: len(mine)]
        return rest[len(mine) :]

    def blocks(self):
        found = []
        for k in range(self.outer):
            at = self.z
            if k:
                at = sum(
                    jnp.where(self.z == z, z - d * far, 0) for z, (far, d) in enumerate(o[k - 1] for o in self.order)
                )
            for j in range(self.inner):
                found.append((at * self.inner + (self.x - j + self.inner) % self.inner, self.held[k][j]))
        return found


def exchange_columns(found, bit):
    pairs = [(i, i ^ bit) for i in range(lax.axis_size("col"))]
    return found + [(far ^ bit, lax.ppermute(x, "col", pairs)) for far, x in found]


def shards(schur, lower, upper, tile_mask, row_map, front):
    children, rows, local_depth = lower.shape
    count = lax.axis_size("row")
    cap = 3 * rows // (2 * count)
    room = cap + NOTES
    row_tiles = rows // TILE
    pairs = local_depth // (2 * TILE)

    relay = Relay(upper, count)
    relay.step()

    target = row_map // rows
    place = row_map % rows
    earlier = jnp.tril(jnp.ones((rows, rows), jnp.bool_), -1)
    rank = jnp.sum((target[:, :, None] == target[:, None, :]) & earlier[None], axis=2, dtype=jnp.int32)
    picks = tile_mask.reshape(children, row_tiles, pairs, 2)[..., 1]
    code = jnp.sum(picks * (2 ** jnp.arange(pairs, dtype=jnp.int32)), axis=-1)
    code = jnp.repeat(code, TILE, axis=1)
    row_ids = jnp.broadcast_to(jnp.arange(rows, dtype=jnp.int32), (children, rows))
    digits = [place // BASE + 1, place % BASE, code, row_ids // BASE, row_ids % BASE]
    digits = [d.astype(jnp.bfloat16) for d in digits] + [row_unit(schur)[..., 0]]
    digits = jnp.stack(digits + [jnp.zeros_like(digits[0])] * (NOTES - len(digits)), axis=1)

    sent_lower = lower_pack(lower, picks, target * room + rank, digits, count, room)
    notes = sent_lower[:, :, cap + 3 : cap + 5, :cap].astype(jnp.int32)
    source = (notes[:, :, 0] * BASE + notes[:, :, 1]).transpose(1, 0, 2).reshape(children, -1)

    sent_lower, source = relay.pass_gate([sent_lower, source])
    relay.step()
    sent = pack(schur, 0, source[0], count, None)
    sent_lower, sent = gate([sent_lower, sent])
    got_lower = lax.all_to_all(sent_lower, "row", split_axis=0, concat_axis=0, tiled=True)
    while relay.k < relay.outer - 2:
        (sent,) = relay.pass_gate([sent])
        relay.step()
    (sent,) = relay.pass_gate([sent])
    relay.step()
    for child in range(1, children):
        sent = pack(schur, child, source[child], count, sent)
    got = lax.all_to_all(sent, "row", split_axis=0, concat_axis=0, tiled=True)

    notes = got_lower[:, :, cap : cap + NOTES, :cap].transpose(2, 1, 0, 3)
    got_place = notes[0].astype(jnp.int32) * BASE + notes[1].astype(jnp.int32) - BASE
    got_place = jnp.where(got_place >= 0, got_place, rows)
    spare = ((0, 0), (0, 0), (0, NOTES))
    full, units = lower_unpack(
        got_lower,
        rows,
        jnp.pad(got_place, spare, constant_values=rows),
        jnp.pad(notes[2].astype(jnp.float32), spare),
        jnp.pad(notes[5].astype(jnp.float32), spare),
    )

    full, units = relay.finish([full, units])
    column = lax.axis_index("col")
    bit = lax.axis_size("col") // 2
    lows = exchange_columns([(0, full)], bit)
    others = relay.finish_along_x([low for _, low in lows])
    lows = [(far, low) for (far, _), low in zip(lows, others)]
    while bit > 1:
        bit //= 2
        lows = exchange_columns(lows, bit)
    ups = relay.blocks()
    starts = [(column ^ far) * local_depth for far, _ in lows] + [owner * upper.shape[1] for owner, _ in ups]
    result = product(front, [low for _, low in lows], [up for _, up in ups], jnp.stack(starts).astype(jnp.int32))
    return unpack(got, got_place, units, result)


def solution(mesh):
    in_specs = (
        P(None, "row", "col"),
        P(None, "row", "col"),
        P(None, "row", "col"),
        P(None, "row", "col"),
        P(None, "row"),
        P("row", "col"),
    )
    out_specs = P("row", "col")
    return jax.shard_map(shards, mesh=mesh, in_specs=in_specs, out_specs=out_specs, check_vma=False)
```

```python
import functools

import jax
import jax.numpy as jnp
from jax import lax
from jax.experimental import pallas as pl
from jax.experimental.pallas import tpu as pltpu
from jax.sharding import PartitionSpec as P

TILE = 128
LANES = 128
TOP = 32767.0
STEP = (1.0 + 2.0**-7) / TOP
NOTES = 16
BASE = 32
TINY = 1e-33
VMEM_LIMIT = 56 * 1024 * 1024
ANY = pl.BlockSpec(memory_space=pl.ANY)


def inner_factor(count):
    inner = 1
    while (2 * inner) * (2 * inner) <= count:
        inner *= 2
    return inner


def takes(us):
    return pl.CostEstimate(flops=int(us * 4e9), bytes_accessed=int(us * 3.3e6), transcendentals=0)


def gate_kernel(*refs):
    pass


def gate(arrays, *first):
    count = len(arrays)
    return pl.pallas_call(
        gate_kernel,
        out_shape=[jax.ShapeDtypeStruct(x.shape, x.dtype) for x in arrays],
        in_specs=[ANY] * (count + len(first)),
        out_specs=[ANY] * count,
        input_output_aliases={i: i for i in range(count)},
        name="gate",
    )(*arrays, *first)


def row_unit(x):
    most = jnp.max(jnp.abs(x), axis=-1, keepdims=True)
    return jnp.where(most > TINY, most * STEP, 0.0).astype(jnp.bfloat16)


def pack_kernel(groups, steps, source, x, *refs):
    out, held, scale = refs[-3:]
    i = pl.program_id(0)
    rows = x.shape[1]
    targets, _, tiles = out.shape[:3]
    per = 16 // groups

    @pl.when(i < steps)
    def _():
        unit = row_unit(x[0]).astype(jnp.float32)
        scale[...] = jnp.broadcast_to(jnp.where(unit > 0.0, 1.0 / unit, 0.0), scale.shape)

        def body(g, carry):
            at = pl.multiple_of(g * 8, 8)
            inverse = scale[pl.ds(at, 8), :]
            base = (i * rows + at) * groups
            for j in range(groups):
                v = x[0, pl.ds(at, 8), j * LANES : (j + 1) * LANES]
                held[pl.ds(base + j, 8, stride=groups), :] = jnp.floor(v * inverse + 0.5).astype(jnp.int32)
            return carry

        lax.fori_loop(0, rows // 8, body, 0, unroll=4)

    @pl.when(i >= steps)
    def _():
        for target in range(targets):
            start = ((i - steps) * targets + target) * tiles * per

            def body(t, carry):
                parts = []
                for a in range(per):
                    row = pl.multiple_of(source[start + t * per + a] * groups, groups)
                    parts.append(held[pl.ds(row, groups), :])
                out[target, 0, t] = jnp.concatenate(parts, axis=0).astype(jnp.int16)
                return carry

            lax.fori_loop(0, tiles, body, 0, unroll=8)


def pack(x, child, source, count, into, *first):
    children, rows, width = x.shape
    cap = source.shape[0] // count
    groups = width // LANES
    tiles = cap * groups // 16
    steps, out_steps = 2, 4
    first = first if into is None else (into,) + first
    return pl.pallas_call(
        functools.partial(pack_kernel, groups, steps),
        out_shape=jax.ShapeDtypeStruct((count, children, tiles, 16, LANES), jnp.int16),
        grid_spec=pltpu.PrefetchScalarGridSpec(
            num_scalar_prefetch=1,
            grid=(steps + out_steps,),
            in_specs=[pl.BlockSpec((1, rows // steps, width), lambda i, s: (child, jnp.minimum(i, steps - 1), 0))]
            + [ANY] * len(first),
            out_specs=pl.BlockSpec(
                (count // out_steps, 1, tiles, 16, LANES),
                lambda i, s: (jnp.maximum(i - steps, 0), child, 0, 0, 0),
            ),
            scratch_shapes=[
                pltpu.VMEM(((rows + 8) * groups, LANES), jnp.int32),
                pltpu.VMEM((rows // steps, LANES), jnp.float32),
            ],
        ),
        input_output_aliases={} if into is None else {2: 0},
        compiler_params=pltpu.CompilerParams(vmem_limit_bytes=VMEM_LIMIT),
        cost_estimate=takes(10),
        name="pack",
    )(source, x, *first)


def unpack_kernel(groups, parts, row_at, valid, got, before, unit, out, held):
    i = pl.program_id(0)
    children = unit.shape[0]
    per = 16 // groups
    chunk = 16
    tiles = got.shape[2]

    @pl.when(i < parts)
    def _():
        for c, s in [(c, s) for s in range(got.shape[0]) for c in range(children)]:
            device = i * got.shape[0] + s
            number = c * parts * got.shape[0] + device
            base = number * tiles * per

            def body(k, carry):
                for t in range(chunk // per):
                    v = got[s, c, k * (chunk // per) + t].astype(jnp.int32).astype(jnp.float32)
                    for a in range(per):
                        row = pl.multiple_of(row_at[base + k * chunk + t * per + a], groups)
                        held[c, pl.ds(row, groups), :] = v[a * groups : (a + 1) * groups]
                return carry

            lax.fori_loop(0, (valid[number] + chunk - 1) // chunk, body, 0)

    @pl.when(i >= parts)
    def _():
        rows = out.shape[0]

        def body(g, carry):
            at = pl.multiple_of(g * 8, 8)
            base = ((i - parts) * rows + at) * groups
            for j in range(groups):
                cols = pl.ds(j * LANES, LANES)
                total = before[pl.ds(at, 8), cols]
                for c in range(children):
                    total += held[c, pl.ds(base + j, 8, stride=groups), :] * unit[c, pl.ds(at, 8), :]
                out[pl.ds(at, 8), cols] = total
            return carry

        lax.fori_loop(0, rows // 8, body, 0, unroll=2)


def unpack(got, place, unit, before):
    rows, width = before.shape
    count, children, tiles = got.shape[:3]
    groups = width // LANES
    steps, out_steps = count // 4, 2

    def block(i, *_):
        return jnp.maximum(i - steps, 0), 0

    valid = jnp.sum(place < rows, axis=2, dtype=jnp.int32)
    return pl.pallas_call(
        functools.partial(unpack_kernel, groups, steps),
        out_shape=jax.ShapeDtypeStruct((rows, width), jnp.float32),
        grid_spec=pltpu.PrefetchScalarGridSpec(
            num_scalar_prefetch=2,
            grid=(steps + out_steps,),
            in_specs=[
                pl.BlockSpec(
                    (count // steps, children, tiles, 16, LANES), lambda i, *_: (jnp.minimum(i, steps - 1), 0, 0, 0, 0)
                ),
                pl.BlockSpec((rows // out_steps, width), block),
                pl.BlockSpec((children, rows // out_steps, LANES), lambda i, *_: (0, block(i)[0], 0)),
            ],
            out_specs=pl.BlockSpec((rows // out_steps, width), block),
            scratch_shapes=[pltpu.VMEM((children, (rows + 8) * groups, LANES), jnp.float32)],
        ),
        compiler_params=pltpu.CompilerParams(vmem_limit_bytes=VMEM_LIMIT),
        cost_estimate=takes(11),
        name="unpack",
    )((place * groups).reshape(-1), valid.reshape(-1), got, before, unit)


def lower_pack_kernel(picks, low, slot, digits, out, compact):
    c = pl.program_id(0)
    rows, wide = compact.shape
    pairs = wide // TILE
    count, _, room, _ = out.shape
    for i in range(rows // TILE):
        for j in range(pairs):
            column = (2 * j + picks[(c * (rows // TILE) + i) * pairs + j]) * TILE
            at = pl.ds(i * TILE, TILE)
            compact[at, j * TILE : (j + 1) * TILE] = low[0, at, pl.ds(pl.multiple_of(column, TILE), TILE)]

    def body(t, carry):
        ids = lax.broadcasted_iota(jnp.int32, (max(room, wide), rows), 0) + t * room
        hit = jnp.where(slot[0] == ids, 1.0, 0.0).astype(jnp.bfloat16)
        mine = jnp.dot(hit[:room], compact[...], preferred_element_type=jnp.float32)
        out[t, 0] = mine.astype(jnp.bfloat16)
        notes = lax.dot_general(
            digits[0], hit[:wide], (((1,), (1,)), ((), ())), preferred_element_type=jnp.float32
        )
        out[t, 0, room - NOTES :, :] = notes.astype(jnp.bfloat16)
        return carry

    lax.fori_loop(0, count, body, 0)


def lower_pack(lower, picks, slot, digits, count, room):
    children, rows, depth = lower.shape
    wide = depth // 2
    return pl.pallas_call(
        lower_pack_kernel,
        out_shape=jax.ShapeDtypeStruct((count, children, room, wide), jnp.bfloat16),
        grid_spec=pltpu.PrefetchScalarGridSpec(
            num_scalar_prefetch=1,
            grid=(children,),
            in_specs=[
                pl.BlockSpec((1, rows, depth), lambda c, p: (c, 0, 0)),
                pl.BlockSpec((1, 1, rows), lambda c, p: (c, 0, 0)),
                pl.BlockSpec((1, NOTES, rows), lambda c, p: (c, 0, 0)),
            ],
            out_specs=pl.BlockSpec((count, 1, room, wide), lambda c, p: (0, c, 0, 0)),
            scratch_shapes=[pltpu.VMEM((rows, wide), jnp.bfloat16)],
        ),
        compiler_params=pltpu.CompilerParams(vmem_limit_bytes=VMEM_LIMIT),
        cost_estimate=takes(7),
        name="lower_pack",
    )(picks.reshape(-1), lower, slot.reshape(children, 1, rows), digits)


def lower_unpack_kernel(got, place, code, unit, out, units):
    count, _, room, wide = got.shape
    slots = count * room
    rows = out.shape[1]
    step = 256

    def body(t, carry):
        at = pl.multiple_of(t * step, step)
        ids = lax.broadcasted_iota(jnp.int32, (step, slots), 0) + at
        hit = place[0] == ids
        mine = jnp.dot(
            jnp.where(hit, 1.0, 0.0).astype(jnp.bfloat16),
            got[...].reshape(slots, wide),
            preferred_element_type=jnp.float32,
        )
        bits = jnp.sum(jnp.where(hit, code[0], 0.0), axis=1, keepdims=True).astype(jnp.int32)
        row = jnp.sum(jnp.where(hit, unit[0], 0.0), axis=1, keepdims=True)
        units[0, pl.ds(at, step), :] = jnp.broadcast_to(row, (step, LANES))
        for j in range(wide // TILE):
            bit = (bits >> j) & 1
            for s in range(2):
                tile = jnp.where(bit == s, mine[:, j * TILE : (j + 1) * TILE], 0.0)
                out[0, pl.ds(at, step), (2 * j + s) * TILE : (2 * j + s + 1) * TILE] = tile.astype(jnp.bfloat16)
        return carry

    lax.fori_loop(0, rows // step, body, 0)


def lower_unpack(got, rows, *lanes):
    count, children, room, wide = got.shape
    slots = count * room
    lane = pl.BlockSpec((1, 1, slots), lambda c: (c, 0, 0))
    whole = lambda n: pl.BlockSpec((1, rows, n), lambda c: (c, 0, 0))
    return pl.pallas_call(
        lower_unpack_kernel,
        out_shape=(
            jax.ShapeDtypeStruct((children, rows, 2 * wide), jnp.bfloat16),
            jax.ShapeDtypeStruct((children, rows, LANES), jnp.float32),
        ),
        grid=(children,),
        in_specs=[pl.BlockSpec((count, 1, room, wide), lambda c: (0, c, 0, 0))] + [lane] * len(lanes),
        out_specs=(whole(2 * wide), whole(LANES)),
        compiler_params=pltpu.CompilerParams(vmem_limit_bytes=VMEM_LIMIT),
        cost_estimate=takes(5),
        name="lower_unpack",
    )(got, *[x.reshape(children, 1, slots) for x in lanes])


def product_kernel(children, steps, parts, blocks, starts, front, *refs):
    lows, ups = refs[:parts], refs[parts : parts + blocks]
    out, low_all, up_all, sems = refs[parts + blocks :]
    i = pl.program_id(0)
    rows = front.shape[0]
    depth = low_all.shape[1] // children

    @pl.when(i == 0)
    def _():
        copies = []
        for c in range(children):
            for n, low in enumerate(lows):
                at = pl.ds(pl.multiple_of(c * depth + starts[n], low.shape[2]), low.shape[2])
                copies.append(pltpu.make_async_copy(low.at[c], low_all.at[:, at], sems.at[len(copies)]))
            for n, up in enumerate(ups):
                at = pl.ds(pl.multiple_of(c * depth + starts[parts + n], up.shape[1]), up.shape[1])
                copies.append(pltpu.make_async_copy(up.at[c], up_all.at[at], sems.at[len(copies)]))
        for copy in copies:
            copy.start()
        for copy in copies:
            copy.wait()

    here = pl.ds(pl.multiple_of(i * rows, rows), rows)
    out[...] = front[...] - jnp.dot(low_all[here, :], up_all[...], preferred_element_type=jnp.float32)


def product(front, lows, ups, starts):
    rows, width = front.shape
    children = ups[0].shape[0]
    depth = children * sum(up.shape[1] for up in ups)
    steps = 4
    block = pl.BlockSpec((rows // steps, width), lambda i, s: (i, 0))
    return pl.pallas_call(
        functools.partial(product_kernel, children, steps, len(lows), len(ups)),
        out_shape=jax.ShapeDtypeStruct((rows, width), jnp.float32),
        grid_spec=pltpu.PrefetchScalarGridSpec(
            num_scalar_prefetch=1,
            grid=(steps,),
            in_specs=[block] + [ANY] * (len(lows) + len(ups)),
            out_specs=block,
            scratch_shapes=[
                pltpu.VMEM((rows, depth), jnp.bfloat16),
                pltpu.VMEM((depth, width), jnp.bfloat16),
                pltpu.SemaphoreType.DMA((children * (len(lows) + len(ups)),)),
            ],
        ),
        compiler_params=pltpu.CompilerParams(vmem_limit_bytes=VMEM_LIMIT),
        cost_estimate=takes(15),
        name="product",
    )(starts, front, *lows, *ups)


class Relay:
    def __init__(self, block, count):
        self.inner = inner_factor(count)
        self.outer = count // self.inner
        self.z = lax.axis_index("row") // self.inner
        self.x = lax.axis_index("row") % self.inner
        self.up = self.down = block
        self.came = {}
        self.order = [
            [(k, d) for k in range(1, self.outer) for d in (1, -1) if 0 <= z - d * k < self.outer]
            for z in range(self.outer)
        ]
        self.held = [[block] + self.exchange(block, range(self.outer))]
        self.k = 0

    def send(self, x, moves, turn=0):
        n = self.inner
        return lax.ppermute(
            x, "row", [(z * n + i, to * n + (i + turn) % n) for z, to in moves.items() for i in range(n)]
        )

    def exchange(self, x, where):
        return [self.send(x, {z: z for z in where}, j) for j in range(1, self.inner)]

    def choose(self, number, where):
        names = {z: self.order[z][number - 1] for z in where}
        every = sorted(set(names.values()))
        block = self.came[every[0]]
        for name in every[1:]:
            here = functools.reduce(jnp.logical_or, [self.z == z for z in where if names[z] == name])
            block = jnp.where(here, self.came[name], block)
        return block

    def step(self):
        if self.k:
            block = self.choose(self.k, range(self.outer))
            self.held.append([block] + self.exchange(block, range(self.outer)))
        self.k += 1
        last = self.outer - 1
        if self.k == last:
            self.inside = self.choose(last, range(1, last))
            self.at_ends = self.send(self.inside, {1: 0, last - 1: last})
            return
        self.up = self.send(self.up, {z: z + 1 for z in range(self.k - 1, last)})
        self.down = self.send(self.down, {z: z - 1 for z in range(1, last - self.k + 2)})
        self.came[self.k, 1], self.came[self.k, -1] = self.up, self.down

    def pass_gate(self, arrays):
        mine = self.held[self.k - 1][1:]
        count = len(mine)
        self.up, self.down, *rest = gate([self.up, self.down, *mine, *arrays])
        self.came[self.k, 1], self.came[self.k, -1] = self.up, self.down
        self.held[self.k - 1][1:] = rest[:count]
        return rest[count:]

    def finish(self, arrays):
        mine = self.held[-1][1:]
        self.at_ends, *rest = gate([self.at_ends, *mine, *arrays])
        self.held[-1][1:] = rest[: len(mine)]
        block = jnp.where((self.z == 0) | (self.z == self.outer - 1), self.at_ends, self.inside)
        self.held.append([block] + self.exchange(block, range(self.outer)))
        return rest[len(mine) :]

    def finish_along_x(self, arrays):
        mine = self.held[-1][1:]
        rest = gate([*mine, *arrays])
        self.held[-1][1:] = rest[: len(mine)]
        return rest[len(mine) :]

    def blocks(self):
        found = []
        for k in range(self.outer):
            at = self.z
            if k:
                at = sum(
                    jnp.where(self.z == z, z - d * far, 0) for z, (far, d) in enumerate(o[k - 1] for o in self.order)
                )
            for j in range(self.inner):
                found.append((at * self.inner + (self.x - j + self.inner) % self.inner, self.held[k][j]))
        return found


def exchange_columns(found, bit):
    pairs = [(i, i ^ bit) for i in range(lax.axis_size("col"))]
    return found + [(far ^ bit, lax.ppermute(x, "col", pairs)) for far, x in found]


def shards(schur, lower, upper, tile_mask, row_map, front):
    children, rows, local_depth = lower.shape
    count = lax.axis_size("row")
    cap = 3 * rows // (2 * count)
    room = cap + NOTES
    row_tiles = rows // TILE
    pairs = local_depth // (2 * TILE)

    relay = Relay(upper, count)
    relay.step()

    target = row_map // rows
    place = row_map % rows
    earlier = jnp.tril(jnp.ones((rows, rows), jnp.bool_), -1)
    rank = jnp.sum((target[:, :, None] == target[:, None, :]) & earlier[None], axis=2, dtype=jnp.int32)
    picks = tile_mask.reshape(children, row_tiles, pairs, 2)[..., 1]
    code = jnp.sum(picks * (2 ** jnp.arange(pairs, dtype=jnp.int32)), axis=-1)
    code = jnp.repeat(code, TILE, axis=1)
    row_ids = jnp.broadcast_to(jnp.arange(rows, dtype=jnp.int32), (children, rows))
    digits = [place // BASE + 1, place % BASE, code, row_ids // BASE, row_ids % BASE]
    digits = [d.astype(jnp.bfloat16) for d in digits] + [row_unit(schur)[..., 0]]
    digits = jnp.stack(digits + [jnp.zeros_like(digits[0])] * (NOTES - len(digits)), axis=1)

    sent_lower = lower_pack(lower, picks, target * room + rank, digits, count, room)
    notes = sent_lower[:, :, cap + 3 : cap + 5, :cap].astype(jnp.int32)
    source = (notes[:, :, 0] * BASE + notes[:, :, 1]).transpose(1, 0, 2).reshape(children, -1)

    sent_lower, source = relay.pass_gate([sent_lower, source])
    relay.step()
    sent = pack(schur, 0, source[0], count, None)
    sent_lower, sent = gate([sent_lower, sent])
    got_lower = lax.all_to_all(sent_lower, "row", split_axis=0, concat_axis=0, tiled=True)
    while relay.k < relay.outer - 2:
        (sent,) = relay.pass_gate([sent])
        relay.step()
    (sent,) = relay.pass_gate([sent])
    relay.step()
    for child in range(1, children):
        sent = pack(schur, child, source[child], count, sent)
    got = lax.all_to_all(sent, "row", split_axis=0, concat_axis=0, tiled=True)

    notes = got_lower[:, :, cap : cap + NOTES, :cap].transpose(2, 1, 0, 3)
    got_place = notes[0].astype(jnp.int32) * BASE + notes[1].astype(jnp.int32) - BASE
    got_place = jnp.where(got_place >= 0, got_place, rows)
    spare = ((0, 0), (0, 0), (0, NOTES))
    full, units = lower_unpack(
        got_lower,
        rows,
        jnp.pad(got_place, spare, constant_values=rows),
        jnp.pad(notes[2].astype(jnp.float32), spare),
        jnp.pad(notes[5].astype(jnp.float32), spare),
    )

    full, units = relay.finish([full, units])
    column = lax.axis_index("col")
    bit = lax.axis_size("col") // 2
    lows = exchange_columns([(0, full)], bit)
    others = relay.finish_along_x([low for _, low in lows])
    lows = [(far, low) for (far, _), low in zip(lows, others)]
    while bit > 1:
        bit //= 2
        lows = exchange_columns(lows, bit)
    ups = relay.blocks()
    starts = [(column ^ far) * local_depth for far, _ in lows] + [owner * upper.shape[1] for owner, _ in ups]
    result = product(front, [low for _, low in lows], [up for _, up in ups], jnp.stack(starts).astype(jnp.int32))
    return unpack(got, got_place, units, result)


def solution(mesh):
    in_specs = (
        P(None, "row", "col"),
        P(None, "row", "col"),
        P(None, "row", "col"),
        P(None, "row", "col"),
        P(None, "row"),
        P("row", "col"),
    )
    out_specs = P("row", "col")
    return jax.shard_map(shards, mesh=mesh, in_specs=in_specs, out_specs=out_specs, check_vma=False)
```

```python
import functools

import jax
import jax.numpy as jnp
from jax import lax
from jax.experimental import pallas as pl
from jax.experimental.pallas import tpu as pltpu
from jax.sharding import PartitionSpec as P

TILE = 128
LANES = 128
TOP = 32767.0
STEP = (1.0 + 2.0**-7) / TOP
NOTES = 16
BASE = 32
TINY = 1e-33
VMEM_LIMIT = 56 * 1024 * 1024
ANY = pl.BlockSpec(memory_space=pl.ANY)


def inner_factor(count):
    inner = 1
    while (2 * inner) * (2 * inner) <= count:
        inner *= 2
    return inner


def takes(us):
    return pl.CostEstimate(flops=int(us * 4e9), bytes_accessed=int(us * 3.3e6), transcendentals=0)


def gate_kernel(*refs):
    pass


def gate(arrays, *first):
    count = len(arrays)
    return pl.pallas_call(
        gate_kernel,
        out_shape=[jax.ShapeDtypeStruct(x.shape, x.dtype) for x in arrays],
        in_specs=[ANY] * (count + len(first)),
        out_specs=[ANY] * count,
        input_output_aliases={i: i for i in range(count)},
        name="gate",
    )(*arrays, *first)


def row_unit(x):
    most = jnp.max(jnp.abs(x), axis=-1, keepdims=True)
    return jnp.where(most > TINY, most * STEP, 0.0).astype(jnp.bfloat16)


def pack_kernel(groups, steps, source, x, *refs):
    out, held, scale = refs[-3:]
    i = pl.program_id(0)
    rows = x.shape[1]
    targets, _, tiles = out.shape[:3]
    per = 16 // groups

    @pl.when(i < steps)
    def _():
        unit = row_unit(x[0]).astype(jnp.float32)
        scale[...] = jnp.broadcast_to(jnp.where(unit > 0.0, 1.0 / unit, 0.0), scale.shape)

        def body(g, carry):
            at = pl.multiple_of(g * 8, 8)
            inverse = scale[pl.ds(at, 8), :]
            base = (i * rows + at) * groups
            for j in range(groups):
                v = x[0, pl.ds(at, 8), j * LANES : (j + 1) * LANES]
                held[pl.ds(base + j, 8, stride=groups), :] = jnp.floor(v * inverse + 0.5).astype(jnp.int32)
            return carry

        lax.fori_loop(0, rows // 8, body, 0, unroll=4)

    @pl.when(i >= steps)
    def _():
        for target in range(targets):
            start = ((i - steps) * targets + target) * tiles * per

            def body(t, carry):
                parts = []
                for a in range(per):
                    row = pl.multiple_of(source[start + t * per + a] * groups, groups)
                    parts.append(held[pl.ds(row, groups), :])
                out[target, 0, t] = jnp.concatenate(parts, axis=0).astype(jnp.int16)
                return carry

            lax.fori_loop(0, tiles, body, 0, unroll=8)


def pack(x, child, source, count, into, *first):
    children, rows, width = x.shape
    cap = source.shape[0] // count
    groups = width // LANES
    tiles = cap * groups // 16
    steps, out_steps = 2, 4
    first = first if into is None else (into,) + first
    return pl.pallas_call(
        functools.partial(pack_kernel, groups, steps),
        out_shape=jax.ShapeDtypeStruct((count, children, tiles, 16, LANES), jnp.int16),
        grid_spec=pltpu.PrefetchScalarGridSpec(
            num_scalar_prefetch=1,
            grid=(steps + out_steps,),
            in_specs=[pl.BlockSpec((1, rows // steps, width), lambda i, s: (child, jnp.minimum(i, steps - 1), 0))]
            + [ANY] * len(first),
            out_specs=pl.BlockSpec(
                (count // out_steps, 1, tiles, 16, LANES),
                lambda i, s: (jnp.maximum(i - steps, 0), child, 0, 0, 0),
            ),
            scratch_shapes=[
                pltpu.VMEM(((rows + 8) * groups, LANES), jnp.int32),
                pltpu.VMEM((rows // steps, LANES), jnp.float32),
            ],
        ),
        input_output_aliases={} if into is None else {2: 0},
        compiler_params=pltpu.CompilerParams(vmem_limit_bytes=VMEM_LIMIT),
        cost_estimate=takes(10),
        name="pack",
    )(source, x, *first)


def unpack_kernel(groups, pieces, row_at, valid, got, before, unit, out, held, total, units, sems):
    i = pl.program_id(0)
    steps = pl.num_programs(0)
    children = unit.shape[0]
    per = 16 // groups
    chunk = 16
    tiles = got.shape[2]
    inward = [
        pltpu.make_async_copy(before, total, sems.at[pieces]),
        pltpu.make_async_copy(unit, units, sems.at[pieces + 1]),
    ]

    @pl.when(i == 0)
    def _():
        for copy in inward:
            copy.start()

    for c, s in [(c, s) for s in range(got.shape[0]) for c in range(children)]:
        device = i * got.shape[0] + s
        number = c * steps * got.shape[0] + device
        base = number * tiles * per

        def body(k, carry):
            for t in range(chunk // per):
                v = got[s, c, k * (chunk // per) + t].astype(jnp.int32).astype(jnp.float32)
                for a in range(per):
                    row = pl.multiple_of(row_at[base + k * chunk + t * per + a], groups)
                    held[c, pl.ds(row, groups), :] = v[a * groups : (a + 1) * groups]
            return carry

        lax.fori_loop(0, (valid[number] + chunk - 1) // chunk, body, 0)

    @pl.when(i == steps - 1)
    def _():
        for copy in inward:
            copy.wait()
        rows = total.shape[0] // pieces
        outward = []
        for piece in range(pieces):

            def body(g, carry):
                at = pl.multiple_of(piece * rows + g * 8, 8)
                base = at * groups
                for j in range(groups):
                    cols = pl.ds(j * LANES, LANES)
                    value = total[pl.ds(at, 8), cols]
                    for c in range(children):
                        value += held[c, pl.ds(base + j, 8, stride=groups), :] * units[c, pl.ds(at, 8), :]
                    total[pl.ds(at, 8), cols] = value
                return carry

            lax.fori_loop(0, rows // 8, body, 0, unroll=2)
            here = pl.ds(piece * rows, rows)
            outward.append(pltpu.make_async_copy(total.at[here], out.at[here], sems.at[piece]))
            outward[-1].start()
        for copy in outward:
            copy.wait()


def unpack(got, place, unit, before):
    rows, width = before.shape
    count, children, tiles = got.shape[:3]
    groups = width // LANES
    steps, pieces = count // 2, 8
    valid = jnp.sum(place < rows, axis=2, dtype=jnp.int32)
    return pl.pallas_call(
        functools.partial(unpack_kernel, groups, pieces),
        out_shape=jax.ShapeDtypeStruct((rows, width), jnp.float32),
        grid_spec=pltpu.PrefetchScalarGridSpec(
            num_scalar_prefetch=2,
            grid=(steps,),
            in_specs=[
                pl.BlockSpec((count // steps, children, tiles, 16, LANES), lambda i, *_: (i, 0, 0, 0, 0)),
                ANY,
                ANY,
            ],
            out_specs=ANY,
            scratch_shapes=[
                pltpu.VMEM((children, (rows + 8) * groups, LANES), jnp.float32),
                pltpu.VMEM((rows, width), jnp.float32),
                pltpu.VMEM(unit.shape, jnp.float32),
                pltpu.SemaphoreType.DMA((pieces + 2,)),
            ],
        ),
        compiler_params=pltpu.CompilerParams(vmem_limit_bytes=VMEM_LIMIT),
        cost_estimate=takes(11),
        name="unpack",
    )((place * groups).reshape(-1), valid.reshape(-1), got, before, unit)


def lower_pack_kernel(picks, low, slot, digits, out, compact):
    c = pl.program_id(0)
    rows, wide = compact.shape
    pairs = wide // TILE
    count, _, room, _ = out.shape
    for i in range(rows // TILE):
        for j in range(pairs):
            column = (2 * j + picks[(c * (rows // TILE) + i) * pairs + j]) * TILE
            at = pl.ds(i * TILE, TILE)
            compact[at, j * TILE : (j + 1) * TILE] = low[0, at, pl.ds(pl.multiple_of(column, TILE), TILE)]

    def body(t, carry):
        ids = lax.broadcasted_iota(jnp.int32, (max(room, wide), rows), 0) + t * room
        hit = jnp.where(slot[0] == ids, 1.0, 0.0).astype(jnp.bfloat16)
        mine = jnp.dot(hit[:room], compact[...], preferred_element_type=jnp.float32)
        out[t, 0] = mine.astype(jnp.bfloat16)
        notes = lax.dot_general(
            digits[0], hit[:wide], (((1,), (1,)), ((), ())), preferred_element_type=jnp.float32
        )
        out[t, 0, room - NOTES :, :] = notes.astype(jnp.bfloat16)
        return carry

    lax.fori_loop(0, count, body, 0)


def lower_pack(lower, picks, slot, digits, count, room):
    children, rows, depth = lower.shape
    wide = depth // 2
    return pl.pallas_call(
        lower_pack_kernel,
        out_shape=jax.ShapeDtypeStruct((count, children, room, wide), jnp.bfloat16),
        grid_spec=pltpu.PrefetchScalarGridSpec(
            num_scalar_prefetch=1,
            grid=(children,),
            in_specs=[
                pl.BlockSpec((1, rows, depth), lambda c, p: (c, 0, 0)),
                pl.BlockSpec((1, 1, rows), lambda c, p: (c, 0, 0)),
                pl.BlockSpec((1, NOTES, rows), lambda c, p: (c, 0, 0)),
            ],
            out_specs=pl.BlockSpec((count, 1, room, wide), lambda c, p: (0, c, 0, 0)),
            scratch_shapes=[pltpu.VMEM((rows, wide), jnp.bfloat16)],
        ),
        compiler_params=pltpu.CompilerParams(vmem_limit_bytes=VMEM_LIMIT),
        cost_estimate=takes(7),
        name="lower_pack",
    )(picks.reshape(-1), lower, slot.reshape(children, 1, rows), digits)


def lower_unpack_kernel(got, place, code, unit, out, units):
    count, _, room, wide = got.shape
    slots = count * room
    rows = out.shape[1]
    step = 256

    def body(t, carry):
        at = pl.multiple_of(t * step, step)
        ids = lax.broadcasted_iota(jnp.int32, (step, slots), 0) + at
        hit = place[0] == ids
        mine = jnp.dot(
            jnp.where(hit, 1.0, 0.0).astype(jnp.bfloat16),
            got[...].reshape(slots, wide),
            preferred_element_type=jnp.float32,
        )
        bits = jnp.sum(jnp.where(hit, code[0], 0.0), axis=1, keepdims=True).astype(jnp.int32)
        row = jnp.sum(jnp.where(hit, unit[0], 0.0), axis=1, keepdims=True)
        units[0, pl.ds(at, step), :] = jnp.broadcast_to(row, (step, LANES))
        for j in range(wide // TILE):
            bit = (bits >> j) & 1
            for s in range(2):
                tile = jnp.where(bit == s, mine[:, j * TILE : (j + 1) * TILE], 0.0)
                out[0, pl.ds(at, step), (2 * j + s) * TILE : (2 * j + s + 1) * TILE] = tile.astype(jnp.bfloat16)
        return carry

    lax.fori_loop(0, rows // step, body, 0)


def lower_unpack(got, rows, *lanes):
    count, children, room, wide = got.shape
    slots = count * room
    lane = pl.BlockSpec((1, 1, slots), lambda c: (c, 0, 0))
    whole = lambda n: pl.BlockSpec((1, rows, n), lambda c: (c, 0, 0))
    return pl.pallas_call(
        lower_unpack_kernel,
        out_shape=(
            jax.ShapeDtypeStruct((children, rows, 2 * wide), jnp.bfloat16),
            jax.ShapeDtypeStruct((children, rows, LANES), jnp.float32),
        ),
        grid=(children,),
        in_specs=[pl.BlockSpec((count, 1, room, wide), lambda c: (0, c, 0, 0))] + [lane] * len(lanes),
        out_specs=(whole(2 * wide), whole(LANES)),
        compiler_params=pltpu.CompilerParams(vmem_limit_bytes=VMEM_LIMIT),
        cost_estimate=takes(5),
        name="lower_unpack",
    )(got, *[x.reshape(children, 1, slots) for x in lanes])


def product_kernel(children, steps, parts, blocks, starts, front, *refs):
    lows, ups = refs[:parts], refs[parts : parts + blocks]
    out, low_all, up_all, sems = refs[parts + blocks :]
    i = pl.program_id(0)
    rows = front.shape[0]
    depth = low_all.shape[1] // children

    @pl.when(i == 0)
    def _():
        copies = []
        for c in range(children):
            for n, low in enumerate(lows):
                at = pl.ds(pl.multiple_of(c * depth + starts[n], low.shape[2]), low.shape[2])
                copies.append(pltpu.make_async_copy(low.at[c], low_all.at[:, at], sems.at[len(copies)]))
            for n, up in enumerate(ups):
                at = pl.ds(pl.multiple_of(c * depth + starts[parts + n], up.shape[1]), up.shape[1])
                copies.append(pltpu.make_async_copy(up.at[c], up_all.at[at], sems.at[len(copies)]))
        for copy in copies:
            copy.start()
        for copy in copies:
            copy.wait()

    here = pl.ds(pl.multiple_of(i * rows, rows), rows)
    out[...] = front[...] - jnp.dot(low_all[here, :], up_all[...], preferred_element_type=jnp.float32)


def product(front, lows, ups, starts):
    rows, width = front.shape
    children = ups[0].shape[0]
    depth = children * sum(up.shape[1] for up in ups)
    steps = 4
    block = pl.BlockSpec((rows // steps, width), lambda i, s: (i, 0))
    return pl.pallas_call(
        functools.partial(product_kernel, children, steps, len(lows), len(ups)),
        out_shape=jax.ShapeDtypeStruct((rows, width), jnp.float32),
        grid_spec=pltpu.PrefetchScalarGridSpec(
            num_scalar_prefetch=1,
            grid=(steps,),
            in_specs=[block] + [ANY] * (len(lows) + len(ups)),
            out_specs=block,
            scratch_shapes=[
                pltpu.VMEM((rows, depth), jnp.bfloat16),
                pltpu.VMEM((depth, width), jnp.bfloat16),
                pltpu.SemaphoreType.DMA((children * (len(lows) + len(ups)),)),
            ],
        ),
        compiler_params=pltpu.CompilerParams(vmem_limit_bytes=VMEM_LIMIT),
        cost_estimate=takes(15),
        name="product",
    )(starts, front, *lows, *ups)


class Relay:
    def __init__(self, block, count):
        self.inner = inner_factor(count)
        self.outer = count // self.inner
        self.z = lax.axis_index("row") // self.inner
        self.x = lax.axis_index("row") % self.inner
        self.up = self.down = block
        self.came = {}
        self.order = [
            [(k, d) for k in range(1, self.outer) for d in (1, -1) if 0 <= z - d * k < self.outer]
            for z in range(self.outer)
        ]
        self.held = [[block] + self.exchange(block, range(self.outer))]
        self.k = 0

    def send(self, x, moves, turn=0):
        n = self.inner
        return lax.ppermute(
            x, "row", [(z * n + i, to * n + (i + turn) % n) for z, to in moves.items() for i in range(n)]
        )

    def exchange(self, x, where):
        return [self.send(x, {z: z for z in where}, j) for j in range(1, self.inner)]

    def choose(self, number, where):
        names = {z: self.order[z][number - 1] for z in where}
        every = sorted(set(names.values()))
        block = self.came[every[0]]
        for name in every[1:]:
            here = functools.reduce(jnp.logical_or, [self.z == z for z in where if names[z] == name])
            block = jnp.where(here, self.came[name], block)
        return block

    def step(self):
        if self.k:
            block = self.choose(self.k, range(self.outer))
            self.held.append([block] + self.exchange(block, range(self.outer)))
        self.k += 1
        last = self.outer - 1
        if self.k == last:
            self.inside = self.choose(last, range(1, last))
            self.at_ends = self.send(self.inside, {1: 0, last - 1: last})
            return
        self.up = self.send(self.up, {z: z + 1 for z in range(self.k - 1, last)})
        self.down = self.send(self.down, {z: z - 1 for z in range(1, last - self.k + 2)})
        self.came[self.k, 1], self.came[self.k, -1] = self.up, self.down

    def pass_gate(self, arrays):
        mine = self.held[self.k - 1][1:]
        count = len(mine)
        self.up, self.down, *rest = gate([self.up, self.down, *mine, *arrays])
        self.came[self.k, 1], self.came[self.k, -1] = self.up, self.down
        self.held[self.k - 1][1:] = rest[:count]
        return rest[count:]

    def finish(self, arrays):
        mine = self.held[-1][1:]
        self.at_ends, *rest = gate([self.at_ends, *mine, *arrays])
        self.held[-1][1:] = rest[: len(mine)]
        block = jnp.where((self.z == 0) | (self.z == self.outer - 1), self.at_ends, self.inside)
        self.held.append([block] + self.exchange(block, range(self.outer)))
        return rest[len(mine) :]

    def finish_along_x(self, arrays):
        mine = self.held[-1][1:]
        rest = gate([*mine, *arrays])
        self.held[-1][1:] = rest[: len(mine)]
        return rest[len(mine) :]

    def blocks(self):
        found = []
        for k in range(self.outer):
            at = self.z
            if k:
                at = sum(
                    jnp.where(self.z == z, z - d * far, 0) for z, (far, d) in enumerate(o[k - 1] for o in self.order)
                )
            for j in range(self.inner):
                found.append((at * self.inner + (self.x - j + self.inner) % self.inner, self.held[k][j]))
        return found


def exchange_columns(found, bit):
    pairs = [(i, i ^ bit) for i in range(lax.axis_size("col"))]
    return found + [(far ^ bit, lax.ppermute(x, "col", pairs)) for far, x in found]


def shards(schur, lower, upper, tile_mask, row_map, front):
    children, rows, local_depth = lower.shape
    count = lax.axis_size("row")
    cap = 3 * rows // (2 * count)
    room = cap + NOTES
    row_tiles = rows // TILE
    pairs = local_depth // (2 * TILE)

    relay = Relay(upper, count)
    relay.step()

    target = row_map // rows
    place = row_map % rows
    earlier = jnp.tril(jnp.ones((rows, rows), jnp.bool_), -1)
    rank = jnp.sum((target[:, :, None] == target[:, None, :]) & earlier[None], axis=2, dtype=jnp.int32)
    picks = tile_mask.reshape(children, row_tiles, pairs, 2)[..., 1]
    code = jnp.sum(picks * (2 ** jnp.arange(pairs, dtype=jnp.int32)), axis=-1)
    code = jnp.repeat(code, TILE, axis=1)
    row_ids = jnp.broadcast_to(jnp.arange(rows, dtype=jnp.int32), (children, rows))
    digits = [place // BASE + 1, place % BASE, code, row_ids // BASE, row_ids % BASE]
    digits = [d.astype(jnp.bfloat16) for d in digits] + [row_unit(schur)[..., 0]]
    digits = jnp.stack(digits + [jnp.zeros_like(digits[0])] * (NOTES - len(digits)), axis=1)

    sent_lower = lower_pack(lower, picks, target * room + rank, digits, count, room)
    notes = sent_lower[:, :, cap + 3 : cap + 5, :cap].astype(jnp.int32)
    source = (notes[:, :, 0] * BASE + notes[:, :, 1]).transpose(1, 0, 2).reshape(children, -1)

    sent_lower, source = relay.pass_gate([sent_lower, source])
    relay.step()
    sent = pack(schur, 0, source[0], count, None)
    sent_lower, sent = gate([sent_lower, sent])
    got_lower = lax.all_to_all(sent_lower, "row", split_axis=0, concat_axis=0, tiled=True)
    while relay.k < relay.outer - 2:
        (sent,) = relay.pass_gate([sent])
        relay.step()
    (sent,) = relay.pass_gate([sent])
    relay.step()
    for child in range(1, children):
        sent = pack(schur, child, source[child], count, sent)
    got = lax.all_to_all(sent, "row", split_axis=0, concat_axis=0, tiled=True)

    notes = got_lower[:, :, cap : cap + NOTES, :cap].transpose(2, 1, 0, 3)
    got_place = notes[0].astype(jnp.int32) * BASE + notes[1].astype(jnp.int32) - BASE
    got_place = jnp.where(got_place >= 0, got_place, rows)
    spare = ((0, 0), (0, 0), (0, NOTES))
    full, units = lower_unpack(
        got_lower,
        rows,
        jnp.pad(got_place, spare, constant_values=rows),
        jnp.pad(notes[2].astype(jnp.float32), spare),
        jnp.pad(notes[5].astype(jnp.float32), spare),
    )

    full, units = relay.finish([full, units])
    column = lax.axis_index("col")
    bit = lax.axis_size("col") // 2
    lows = exchange_columns([(0, full)], bit)
    others = relay.finish_along_x([low for _, low in lows])
    lows = [(far, low) for (far, _), low in zip(lows, others)]
    while bit > 1:
        bit //= 2
        lows = exchange_columns(lows, bit)
    ups = relay.blocks()
    starts = [(column ^ far) * local_depth for far, _ in lows] + [owner * upper.shape[1] for owner, _ in ups]
    result = product(front, [low for _, low in lows], [up for _, up in ups], jnp.stack(starts).astype(jnp.int32))
    return unpack(got, got_place, units, result)


def solution(mesh):
    in_specs = (
        P(None, "row", "col"),
        P(None, "row", "col"),
        P(None, "row", "col"),
        P(None, "row", "col"),
        P(None, "row"),
        P("row", "col"),
    )
    out_specs = P("row", "col")
    return jax.shard_map(shards, mesh=mesh, in_specs=in_specs, out_specs=out_specs, check_vma=False)
```
